512 devices in a mesh: segment: 4 (over x), patch: 128 (over z, y, core).
Axes of the slice: x: 4, y: 8, z: 8, core: 2. Of those that a mesh axis runs over, the one named last changes fastest.
Arguments:
- x_in: bfloat16 [8192, 1536], P('patch'), may hold values from -6 to 6
- stale_kv: bfloat16 [4, 8192, 1536], P('segment', 'patch'), may hold values from -6 to 6
- owner: int32 [32, 16], replicated, may hold values from 0 to 15, each once within a row
- live: int32 [128], P('patch'), may hold values from 1 to 4, as said below
- gain: float32 [4, 1536], P('segment'), may hold values from 0.5 to 1.5
- qk_gain: float32 [4, 2, 64], P('segment'), may hold values from 0.5 to 1.5
- w_qkv: bfloat16 [4, 1536, 2304], P('segment', 'patch'), may hold values from -0.15625 to 0.15625
- w_out: bfloat16 [4, 768, 1536], P('segment', None, 'patch'), may hold values from -0.875 to 0.875
Outputs:
- sections: bfloat16 [4, 8192, 1536], P('segment', 'patch')
The draws below stay inside these ranges and needn't reach their ends.
Inputs may be any that keep to these rules, and one draw needn't show every extreme that they name: `live`: every device denoises its first one or more micro-patches, and some device all 4. `owner`: each row holds every patch number of one image once.
All inputs are finite; a program needn't handle non-finite values.
Results may differ from the reference program's by a relative error of at most 0.023.
Values may be sent and summed in bfloat16 or wider, within the bound.
A program may use at most 64 MiB of HBM per device.

```python
import jax
import jax.numpy as jnp
from jax import lax

D = 1536
HEADS = 12
HEAD = 64
MICRO = 4
MROWS = 16
IMG = 256
PATCHES = 16
IMAGES = 32
TOKENS = 8192
HD = 768
N_SEGMENT = 4
N_PATCH = 128


def draw_live(key, part):
    key = jax.random.fold_in(key, 7)
    first_key, second_key = jax.random.split(key)
    counts = jax.random.randint(first_key, (N_PATCH,), 1, MICRO + 1)
    chosen = jax.random.randint(second_key, (), 0, N_PATCH)
    return jnp.where(jnp.arange(N_PATCH) == chosen, MICRO, counts).astype(jnp.int32)


def level_of(stream_key, dims, shards, low, top_value):
    def one(dim, blocks):
        heights = jax.random.uniform(jax.random.fold_in(jax.random.fold_in(stream_key, 6), dim), (blocks,), jnp.float32, low / len(shards), top_value / len(shards))
        return jnp.repeat(jnp.exp(heights), dims[dim] // blocks).reshape((-1,) + (1,) * (len(dims) - dim - 1))

    factor_of = one(*shards[0])
    for cut in shards[1:]:
        factor_of = factor_of * one(*cut)
    return factor_of


def normal_values(key, extent, scale, reach, cuts=(), held_as=jnp.bfloat16):
    entries = jax.random.normal(key, extent, jnp.float32) * scale
    if len(cuts) > 0:
        entries = level_of(key, extent, cuts, -0.22, 0.18) * entries
    return jnp.clip(entries, min=-reach, max=reach).astype(held_as)


def setup_inputs(seed: int = 0) -> dict:
    streams_of = jax.random.split(jax.random.key(seed), 9)
    return {
        "x_in": normal_values(streams_of[0], (TOKENS, D), 1.0, 6.0, ((0, 128),)),
        "stale_kv": normal_values(streams_of[1], (N_SEGMENT, TOKENS, 2 * HD), 1.0, 6.0, ((0, 4), (1, 128))),
        "owner": jax.vmap(lambda own: jax.random.permutation(own, PATCHES))(jax.random.split(streams_of[2], IMAGES)).reshape((IMAGES, PATCHES)).astype(jnp.int32),
        "live": draw_live(jax.random.fold_in(streams_of[8], 71), 0),
        "gain": jnp.clip(0.5 + 1.0 * jax.random.uniform(streams_of[4], (N_SEGMENT, D), jnp.float32) ** level_of(streams_of[4], (N_SEGMENT, D), ((0, 4),), -0.2, 0.2), 0.5, 1.5),
        "qk_gain": jnp.clip(0.5 + 1.0 * jax.random.uniform(streams_of[5], (N_SEGMENT, 2, HEAD), jnp.float32) ** level_of(streams_of[5], (N_SEGMENT, 2, HEAD), ((0, 4),), -0.2, 0.2), 0.5, 1.5),
        "w_qkv": normal_values(streams_of[6], (N_SEGMENT, D, 3 * HD), D ** -0.5, 0.15625, ((0, 4), (1, 128))),
        "w_out": normal_values(streams_of[7], (N_SEGMENT, HD, D), (HD // 16) ** -0.5, 0.875, ((0, 4), (2, 128))),
    }


def rounded(values):
    return lax.optimization_barrier(values.astype(jnp.bfloat16)).astype(jnp.float32)

def scaled_rms(values, gain_row):
    return values * lax.rsqrt(lax.optimization_barrier(jnp.mean(values * values, -1, keepdims=True)) + 1e-06) * gain_row

def section_ref(current, gain_row, head_gains, w_in, w_back, stale_rows, owner, is_live):
    widened = current.astype(jnp.float32)
    normed = scaled_rms(widened, gain_row).astype(jnp.bfloat16)
    fresh_rows = jnp.dot(normed, w_in, preferred_element_type=jnp.float32).astype(jnp.bfloat16)
    key_patch = jnp.arange(IMG, dtype=jnp.int32) // MROWS
    score_scale = HEAD ** (-0.5)

    def one_micro(index):
        image = (index // PATCHES).astype(jnp.int32)
        local = (index % PATCHES).astype(jnp.int32)
        first = (index * MROWS).astype(jnp.int32)
        block = lax.dynamic_slice_in_dim(fresh_rows, first, MROWS, 0).astype(jnp.float32)
        queries = rounded(scaled_rms(block[:, :HD].reshape(MROWS, HEADS, HEAD), head_gains[0]))
        own_keys = rounded(scaled_rms(block[:, HD:2 * HD].reshape(MROWS, HEADS, HEAD), head_gains[1]))
        own_vals = block[:, 2 * HD:].reshape(MROWS, HEADS, HEAD)
        start = (image * IMG).astype(jnp.int32)
        context = lax.dynamic_slice_in_dim(stale_rows, start, IMG, 0).astype(jnp.float32)
        stale_keys = context[:, :HD].reshape(IMG, HEADS, HEAD)
        stale_vals = context[:, HD:].reshape(IMG, HEADS, HEAD)
        patch_id = owner[image, local]
        far_exp = jnp.exp(jnp.einsum('qhd,khd->hqk', queries, stale_keys) * score_scale)
        far_exp = jnp.where(key_patch[None, None, :] == patch_id, jnp.zeros_like(far_exp), far_exp)
        own_exp = jnp.exp(jnp.einsum('qhd,khd->hqk', queries, own_keys) * score_scale)
        row_total = far_exp.sum(-1) + own_exp.sum(-1)
        weighted = jnp.einsum('hqk,khd->qhd', rounded(far_exp), stale_vals)
        weighted = weighted + jnp.einsum('hqk,khd->qhd', rounded(own_exp), own_vals)
        return (weighted / row_total.T[:, :, None]).reshape(MROWS, HD).astype(jnp.bfloat16)
    attended = lax.map(one_micro, jnp.arange(N_PATCH * MICRO, dtype=jnp.int32)).reshape(TOKENS, HD)
    projected = jnp.dot(attended, w_back, preferred_element_type=jnp.float32)
    return jnp.where(is_live[:, None], widened + projected, widened).astype(jnp.bfloat16)

def reference(x_in, stale_kv, owner, live, gain, qk_gain, w_qkv, w_out):
    micro_index = jnp.arange(TOKENS, dtype=jnp.int32) // MROWS
    is_live = micro_index % MICRO < live[micro_index // MICRO]
    current = x_in
    results = []
    for section in range(N_SEGMENT):
        current = section_ref(current, gain[section], qk_gain[section], w_qkv[section], w_out[section], stale_kv[section], owner, is_live)
        results.append(current)
    return jnp.stack(results)
```

```python
import functools

import jax
import jax.numpy as jnp
from jax import lax
from jax.experimental import pallas as pl
from jax.experimental.pallas import tpu as pltpu
from jax.sharding import PartitionSpec as P

MESH = pl.DeviceIdType.MESH
BF = jnp.bfloat16
F32 = jnp.float32

SEG = 4
NZ = 8
NY = 8
GROUP = 4
SHARD = 12
SLOT = 16
BLOCK = GROUP * SHARD
ROWS = 64
MROWS = 16
MICRO = 4
IMG = GROUP * ROWS
HEAD = 64
GH = 3
GW = GH * HEAD
PIECE = 2 * GW
D = 1536
HD = 768
LONG = NZ // 2
SHORT = NZ - 1 - LONG


def kernel(
    x_ref, stale_ref, owner_ref, live_ref, gain_ref, qkg_ref, wqkv_ref, wout_ref,
    out_ref,
    wsend, stg, blk, w, stsend, st, gains, qkgs, xs, rs_out, rs_in, own_part,
    wst_s, wst_r, g_s, g_r, qg_s, qg_r, st_s, st_r, y_s, y_r,
    rl_s, rl_r, sh_s, sh_r, m_s, m_r, rs_s, rs_r, ag_s, ag_r, loc,
):
    c = lax.axis_index("segment")
    p = lax.axis_index("patch")
    image = p // GROUP
    j = p % GROUP
    core = p % 2
    y = (p // 2) % NY
    z = p // (2 * NY)
    yp = y // 2
    mate = p + 1 - 2 * core

    def dev(seg, patch):
        return (seg, patch)

    def patch_of(zz, yy, cc):
        return zz * (2 * NY) + yy * 2 + cc

    barrier = pltpu.get_barrier_semaphore()
    partners = []
    for dc in range(SEG):
        for dj in range(GROUP):
            if dc or dj:
                partners.append(dev((c + dc) % SEG, image * GROUP + (j + dj) % GROUP))
    for dy in range(1, NY // 2):
        pair = (yp + dy) % (NY // 2)
        for low in range(4):
            partners.append(dev(c, z * (2 * NY) + pair * 4 + low))
    step = 1 - 2 * core
    z_long = (z + step + NZ) % NZ
    z_short = (z - step + NZ) % NZ
    partners.append(dev(c, patch_of(z_long, y, core)))
    partners.append(dev(c, patch_of(z_short, y, core)))
    for partner in partners:
        pl.semaphore_signal(barrier, inc=1, device_id=partner, device_id_type=MESH)

    wsend[...] = jnp.zeros_like(wsend)
    for g in range(SEG):
        for part in range(3):
            wsend[g, 0:SHARD, part * GW : (part + 1) * GW] = wqkv_ref[
                :, part * HD + g * GW : part * HD + (g + 1) * GW
            ]
        wsend[g, 0:SHARD, 3 * GW :] = wout_ref[:, g * GW : (g + 1) * GW]
        for part in range(2):
            stsend[g, :, part * GW : (part + 1) * GW] = stale_ref[
                :, part * HD + g * GW : part * HD + (g + 1) * GW
            ]
    for g in range(SEG):
        xs[0, g] = x_ref[:, g * PIECE : (g + 1) * PIECE]
    gains[c] = gain_ref[...]
    qkgs[c] = qkg_ref[...]
    pl.semaphore_wait(barrier, len(partners))

    def remote(src, dst, ss, rs, device):
        return pltpu.make_async_remote_copy(
            src_ref=src, dst_ref=dst, send_sem=ss, recv_sem=rs,
            device_id=device, device_id_type=MESH,
        )

    def stage(d):
        g = (c + d) % SEG
        return remote(
            wsend.at[g], stg.at[j], wst_s.at[d], wst_r.at[j], dev(g, image * GROUP + c)
        )

    def stage_local():
        return pltpu.make_async_copy(wsend.at[c], stg.at[j], wst_r.at[j])

    for d in range(1, SEG):
        stage(d).start()

    @pl.when(j == c)
    def _():
        stage_local().start()

    @pl.when(j != c)
    def _():
        stage(0).start()

    def gain_copy(d):
        return remote(gain_ref, gains.at[c], g_s.at[d - 1], g_r.at[d - 1], dev((c + d) % SEG, p))

    def qkg_copy(d):
        return remote(qkg_ref, qkgs.at[c], qg_s.at[d - 1], qg_r.at[d - 1], dev((c + d) % SEG, p))

    for d in range(1, SEG):
        gain_copy(d).start()
        qkg_copy(d).start()

    def stale_copy(dc, dj):
        g = (c + dc) % SEG
        return remote(
            stsend.at[g], st.at[c, j], st_s.at[dc * GROUP + dj], st_r.at[c],
            dev(g, image * GROUP + (j + dj) % GROUP),
        )

    pltpu.make_async_copy(stsend.at[c], st.at[c, j], st_r.at[c]).start()
    for dj in range(GROUP):
        for dc in range(SEG):
            if dc or dj:
                stale_copy(dc, dj).start()

    for slot in range(GROUP):
        pltpu.make_async_copy(wsend.at[0], stg.at[slot], wst_r.at[slot]).wait()
    a = lax.broadcasted_iota(jnp.int32, (BLOCK, GROUP * SLOT), 0)
    b = lax.broadcasted_iota(jnp.int32, (BLOCK, GROUP * SLOT), 1)
    pick = jnp.zeros((BLOCK, GROUP * SLOT), F32)
    for slot in range(GROUP):
        hit = (a - SHARD * slot == b - SLOT * slot) & (b >= SLOT * slot) & (b < SLOT * slot + SHARD)
        pick = jnp.where(hit, 1.0, pick)
    packed = jnp.dot(
        pick.astype(BF), stg[...].reshape(GROUP * SLOT, 2 * PIECE), preferred_element_type=F32
    ).astype(BF)
    blk[0] = packed[:, :PIECE]
    blk[1] = packed[:, PIECE:]

    def y_copy(dy, piece):
        target = patch_of(z, (y + dy) % NY, piece)
        return remote(
            blk.at[piece], w.at[j, piece, z, yp], y_s.at[dy * 2 + piece], y_r.at[j], dev(c, target)
        )

    def y_mate():
        return remote(
            blk.at[1 - core], w.at[j, 1 - core, z, yp], y_s.at[0], y_r.at[j], dev(c, mate)
        )

    def y_start(s):
        @pl.when(j == s)
        def _():
            pltpu.make_async_copy(blk.at[core], w.at[j, core, z, yp], y_r.at[j]).start()
            y_mate().start()
            for dy in (1, 7, 2, 6, 3, 5, 4):
                for piece in range(2):
                    y_copy(dy, piece).start()

    def ring(s, t, way):
        if way == 0:
            source, target, ss, rs = z - step * t, z_long, rl_s, rl_r
        else:
            source, target, ss, rs = z + step * t, z_short, sh_s, sh_r
        block = w.at[s, core, (source + NZ) % NZ]
        return remote(block, block, ss.at[s, t], rs.at[s, t], dev(c, patch_of(target, y, core)))

    def to_mate(s, t, way):
        source = z - step * t if way == 0 else z + step * t
        block = w.at[s, core, (source + NZ) % NZ]
        index = t if way == 0 else LONG + t
        return remote(block, block, m_s.at[s, index], m_r.at[s], dev(c, mate))

    def ring_wait(s, t, way):
        source = z - step * t if way == 0 else z + step * t
        block = w.at[s, core, (source + NZ) % NZ]
        rs = rl_r if way == 0 else sh_r
        pltpu.make_async_copy(block, block, rs.at[s, t - 1]).wait()

    def ring_start(s):
        block = w.at[s, core, z]
        pltpu.make_async_copy(block, block, y_r.at[s]).wait()
        ring(s, 0, 0).start()
        ring(s, 0, 1).start()
        to_mate(s, 0, 0).start()

    def ring_round(s, t):
        for way, hops in ((0, LONG), (1, SHORT)):
            if t <= hops:
                ring_wait(s, t, way)
                if t < hops:
                    ring(s, t, way).start()
                to_mate(s, t, way).start()

    y_start(0)
    ring_start(0)
    y_start(1)
    ring_round(0, 1)
    y_start(2)
    ring_round(0, 2)
    y_start(3)
    ring_round(0, 3)
    ring_start(1)
    ring_round(0, 4)

    lane_g = lax.broadcasted_iota(jnp.int32, (1, GW), 1)
    head_of = [(lane_g >= h * HEAD) & (lane_g < (h + 1) * HEAD) for h in range(GH)]
    lane_w = lax.broadcasted_iota(jnp.int32, (1, 256), 1)
    head_in_window = [(lane_w >= 64 + h * HEAD) & (lane_w < 64 + (h + 1) * HEAD) for h in range(GH)]
    row = lax.broadcasted_iota(jnp.int32, (ROWS, IMG), 0)
    key_row = lax.broadcasted_iota(jnp.int32, (ROWS, IMG), 1)
    barred = jnp.zeros((ROWS, IMG), jnp.int32)
    live_count = live_ref[0]
    for m in range(MICRO):
        first = owner_ref[image, j * MICRO + m] * MROWS
        hit = (row >= m * MROWS) & (row < (m + 1) * MROWS) & (key_row >= first) & (key_row < first + MROWS)
        barred = jnp.where(hit, 1, barred)
    far_mask = jnp.where(barred == 1, 0.0, 1.0)
    far_mask = jnp.concatenate([far_mask] * GH, 0)
    own_r = lax.broadcasted_iota(jnp.int32, (ROWS, ROWS), 0)
    own_k = lax.broadcasted_iota(jnp.int32, (ROWS, ROWS), 1)
    own_mask = jnp.zeros((ROWS, ROWS), F32)
    for m in range(MICRO):
        lo, hi = m * MROWS, (m + 1) * MROWS
        own_mask = jnp.where((own_r >= lo) & (own_r < hi) & (own_k >= lo) & (own_k < hi), 1.0, own_mask)
    own_mask = jnp.concatenate([own_mask] * GH, 0)
    row1 = lax.broadcasted_iota(jnp.int32, (ROWS, 1), 0)
    live_rows = jnp.where(row1 < live_count * MROWS, 1.0, 0.0)
    live_rows = jnp.concatenate([live_rows] * GH, 0)

    def head_norm(part, gain_row):
        squares = part * part
        scale = jnp.zeros_like(part)
        for h in range(GH):
            mean = jnp.sum(jnp.where(head_of[h], squares, 0.0), -1, keepdims=True) * (1.0 / HEAD)
            scale = jnp.where(head_of[h], lax.rsqrt(mean + 1e-06), scale)
        return part * scale * gain_row

    def nt(lhs, rhs):
        return lax.dot_general(lhs, rhs, (((1,), (1,)), ((), ())), preferred_element_type=F32)

    def chain_front(s):
        other = 1 - core
        pltpu.make_async_copy(w.at[s, other], w.at[s, other], m_r.at[s]).wait()
        if s == 0:
            for d in range(1, SEG):
                src = (c + SEG - d) % SEG
                pltpu.make_async_copy(gain_ref, gains.at[src], g_r.at[d - 1]).wait()
                pltpu.make_async_copy(qkg_ref, qkgs.at[src], qg_r.at[d - 1]).wait()
        else:
            for d in range(1, SEG):
                src = (c + SEG - d) % SEG
                pltpu.make_async_copy(xs.at[s, src], xs.at[s, src], ag_r.at[s - 1, d - 1]).wait()
        x = jnp.concatenate([xs[s, g] for g in range(SEG)], 1).astype(F32)
        inverse = lax.rsqrt(jnp.mean(x * x, -1, keepdims=True) + 1e-06)
        normed = (x * inverse * gains[s]).astype(BF)
        qk = jnp.dot(normed, w[s, 0].reshape(D, PIECE), preferred_element_type=F32).astype(BF).astype(F32)
        value = jnp.dot(normed, w[s, 1].reshape(D, PIECE), preferred_element_type=F32).astype(BF)
        gq = qkgs[s, 0:1, :]
        gk = qkgs[s, 1:2, :]
        query = head_norm(qk[:, :GW], jnp.concatenate([gq] * GH, 1))
        key = head_norm(qk[:, GW:], jnp.concatenate([gk] * GH, 1)).astype(BF)
        query = query.astype(BF).astype(F32)
        stacked = jnp.concatenate([jnp.where(head_of[h], query, 0.0) for h in range(GH)], 0).astype(BF)
        pltpu.make_async_copy(st.at[s], st.at[s], st_r.at[s]).wait()
        kv = st[s].reshape(IMG, PIECE)
        scale = HEAD**-0.5
        far = jnp.exp(nt(stacked, kv[:, :GW]) * scale) * far_mask
        own = jnp.exp(nt(stacked, key) * scale) * own_mask
        total = jnp.sum(far, -1, keepdims=True) + jnp.sum(own, -1, keepdims=True)
        value_window = jnp.concatenate([jnp.zeros((ROWS, 64), F32), value[:, :GW].astype(F32)], 1).astype(BF)
        weighted = jnp.dot(far.astype(BF), kv[:, PIECE - 256 :], preferred_element_type=F32)
        weighted = weighted + jnp.dot(own.astype(BF), value_window, preferred_element_type=F32)
        weighted = weighted * (live_rows / total)
        attended = jnp.zeros((ROWS, 256), F32)
        for h in range(GH):
            attended = jnp.where(head_in_window[h], weighted[h * ROWS : (h + 1) * ROWS], attended)
        attended = attended.astype(BF)
        for d in (1, 2, 3, 0):
            g = (c + d) % SEG
            rows = w[s, 1, pl.ds(2 * g, 2), :, :, PIECE - 256 :].reshape(PIECE, 256)
            part = nt(attended, rows)
            if d:
                rs_out[s, d - 1] = part.astype(BF)
                rs_copy(s, d).start()
            else:
                own_part[...] = part

    def rs_copy(s, d):
        return remote(
            rs_out.at[s, d - 1], rs_in.at[s, d - 1], rs_s.at[s, d - 1], rs_r.at[s, d - 1],
            dev((c + d) % SEG, p),
        )

    def ag_copy(s, d):
        return remote(
            xs.at[s + 1, c], xs.at[s + 1, c], ag_s.at[s, d - 1], ag_r.at[s, d - 1],
            dev((c + d) % SEG, p),
        )

    def chain_back(s):
        for d in range(1, SEG):
            pltpu.make_async_copy(rs_in.at[s, d - 1], rs_in.at[s, d - 1], rs_r.at[s, d - 1]).wait()
        total = own_part[...]
        for d in range(1, SEG):
            total = total + rs_in[s, d - 1].astype(F32)
        xs[s + 1, c] = (xs[s, c].astype(F32) + total).astype(BF)
        for d in range(1, SEG):
            ag_copy(s, d).start()

    for s in range(SEG):
        chain_front(s)
        if s + 1 < SEG:
            ring_round(s + 1, 1)
        chain_back(s)
        if s + 1 < SEG:
            ring_round(s + 1, 2)
            ring_round(s + 1, 3)
            if s + 2 < SEG:
                ring_start(s + 2)
            ring_round(s + 1, 4)

    for d in range(1, SEG):
        src = (c + SEG - d) % SEG
        pltpu.make_async_copy(xs.at[SEG, src], xs.at[SEG, src], ag_r.at[SEG - 1, d - 1]).wait()
    for g in range(SEG):
        out_ref[0, :, g * PIECE : (g + 1) * PIECE] = xs[c + 1, g]

    for d in range(1, SEG):
        stage(d).wait_send()
        gain_copy(d).wait_send()
        qkg_copy(d).wait_send()

    @pl.when(j != c)
    def _():
        stage(0).wait_send()

    for dj in range(GROUP):
        for dc in range(SEG):
            if dc or dj:
                stale_copy(dc, dj).wait_send()
    y_mate().wait_send()
    for dy in range(1, NY):
        for piece in range(2):
            y_copy(dy, piece).wait_send()
    for s in range(SEG):
        for way, hops in ((0, LONG), (1, SHORT)):
            for t in range(hops):
                ring(s, t, way).wait_send()
            for t in range(way, hops + 1):
                to_mate(s, t, way).wait_send()
        for d in range(1, SEG):
            rs_copy(s, d).wait_send()
            ag_copy(s, d).wait_send()


def per_device(x_in, stale_kv, owner, live, gain, qk_gain, w_qkv, w_out):
    vmem = pl.BlockSpec(memory_space=pltpu.VMEM)
    smem = pl.BlockSpec(memory_space=pltpu.SMEM)
    dma = pltpu.SemaphoreType.DMA
    return pl.pallas_call(
        kernel,
        out_shape=jax.ShapeDtypeStruct((1, ROWS, D), BF),
        in_specs=[vmem, vmem, smem, smem, vmem, vmem, vmem, vmem],
        out_specs=vmem,
        scratch_shapes=[
            pltpu.VMEM((SEG, SLOT, 2 * PIECE), BF),
            pltpu.VMEM((GROUP, SLOT, 2 * PIECE), BF),
            pltpu.VMEM((2, BLOCK, PIECE), BF),
            pltpu.VMEM((SEG, 2, NZ, NY // 2, BLOCK, PIECE), BF),
            pltpu.VMEM((SEG, ROWS, PIECE), BF),
            pltpu.VMEM((SEG, GROUP, ROWS, PIECE), BF),
            pltpu.VMEM((SEG, 1, D), F32),
            pltpu.VMEM((SEG, 2, HEAD), F32),
            pltpu.VMEM((SEG + 1, SEG, ROWS, PIECE), BF),
            pltpu.VMEM((SEG, SEG - 1, ROWS, PIECE), BF),
            pltpu.VMEM((SEG, SEG - 1, ROWS, PIECE), BF),
            pltpu.VMEM((ROWS, PIECE), F32),
            dma((SEG,)), dma((GROUP,)),
            dma((SEG - 1,)), dma((SEG - 1,)), dma((SEG - 1,)), dma((SEG - 1,)),
            dma((SEG * GROUP,)), dma((SEG,)),
            dma((2 * NY,)), dma((SEG,)),
            dma((SEG, LONG)), dma((SEG, LONG)), dma((SEG, SHORT)), dma((SEG, SHORT)),
            dma((SEG, NZ)), dma((SEG,)),
            dma((SEG, SEG - 1)), dma((SEG, SEG - 1)), dma((SEG, SEG - 1)), dma((SEG, SEG - 1)),
            dma((1,)),
        ],
        compiler_params=pltpu.CompilerParams(
            collective_id=0, has_side_effects=True, vmem_limit_bytes=40 * 2**20
        ),
    )(x_in, stale_kv[0], owner, live, gain, qk_gain[0], w_qkv[0], w_out[0].T)


def solution(mesh):
    in_specs = (
        P("patch", None),
        P("segment", "patch", None),
        P(),
        P("patch"),
        P("segment", None),
        P("segment", None, None),
        P("segment", "patch", None),
        P("segment", None, "patch"),
    )
    return jax.shard_map(
        per_device, mesh=mesh, in_specs=in_specs, out_specs=P("segment", "patch", None), check_vma=False
    )
```

```python
import functools

import jax
import jax.numpy as jnp
from jax import lax
from jax.experimental import pallas as pl
from jax.experimental.pallas import tpu as pltpu
from jax.sharding import PartitionSpec as P

MESH = pl.DeviceIdType.MESH
BF = jnp.bfloat16
F32 = jnp.float32

SEG = 4
NZ = 8
NY = 8
GROUP = 4
SHARD = 12
SLOT = 16
BLOCK = GROUP * SHARD
ROWS = 64
MROWS = 16
MICRO = 4
IMG = GROUP * ROWS
HEAD = 64
GH = 3
GW = GH * HEAD
PIECE = 2 * GW
D = 1536
HD = 768
LONG = NZ // 2
SHORT = NZ - 1 - LONG


def kernel(
    x_hbm, stale_hbm, owner_ref, live_ref, gain_hbm, qkg_hbm, wqkv_hbm, wout_hbm,
    out_ref,
    x_ref, stale_ref, gain_ref, qkg_ref, wqkv_ref, wout_ref,
    wsend, stg, blk, w, stsend, st, gains, qkgs, xs, rs_out, rs_in, own_part,
    in_sem, wst_s, wst_r, g_s, g_r, qg_s, qg_r, st_s, st_r, y_s, y_r,
    rl_s, rl_r, sh_s, sh_r, m_s, m_r, rs_s, rs_r, ag_s, ag_r,
):
    c = lax.axis_index("segment")
    p = lax.axis_index("patch")
    image = p // GROUP
    j = p % GROUP
    core = p % 2
    y = (p // 2) % NY
    z = p // (2 * NY)
    yp = y // 2
    zh = z // 4
    mate = p + 1 - 2 * core

    def dev(seg, patch):
        return (seg, patch)

    def patch_of(zz, yy, cc):
        return zz * (2 * NY) + yy * 2 + cc

    inputs = [
        pltpu.make_async_copy(src, dst, in_sem.at[n])
        for n, (src, dst) in enumerate(
            [
                (wqkv_hbm, wqkv_ref), (wout_hbm, wout_ref), (stale_hbm, stale_ref),
                (gain_hbm, gain_ref), (qkg_hbm, qkg_ref), (x_hbm, x_ref),
            ]
        )
    ]
    for copy in inputs:
        copy.start()

    barrier = pltpu.get_barrier_semaphore()
    partners = []
    for dc in range(SEG):
        for dj in range(GROUP):
            if dc or dj:
                partners.append(dev((c + dc) % SEG, image * GROUP + (j + dj) % GROUP))
    for dy in range(1, NY // 2):
        pair = (yp + dy) % (NY // 2)
        for low in range(4):
            partners.append(dev(c, z * (2 * NY) + pair * 4 + low))
    for dz in range(1, NZ):
        for low in range(2):
            partners.append(dev(c, patch_of((z + dz) % NZ, y, low)))
    for partner in partners:
        pl.semaphore_signal(barrier, inc=1, device_id=partner, device_id_type=MESH)

    wsend[...] = jnp.zeros_like(wsend)
    inputs[0].wait()
    inputs[1].wait()
    for g in range(SEG):
        for part in range(3):
            wsend[part // 2, g, 0:SHARD, part % 2 * GW : (part % 2 + 1) * GW] = wqkv_ref[
                :, part * HD + g * GW : part * HD + (g + 1) * GW
            ]
        wsend[1, g, 0:SHARD, GW:] = wout_ref[:, g * GW : (g + 1) * GW]
    pl.semaphore_wait(barrier, len(partners))

    def remote(src, dst, ss, rs, device):
        return pltpu.make_async_remote_copy(
            src_ref=src, dst_ref=dst, send_sem=ss, recv_sem=rs,
            device_id=device, device_id_type=MESH,
        )

    holder = [2 * (1 - zh) + c % 2, 2 * zh + c % 2]
    holds_a = y % 2 != zh

    def stage(d, piece):
        g = (c + d) % SEG
        return remote(
            wsend.at[piece, g], stg.at[c // 2, j], wst_s.at[d, piece], wst_r.at[c // 2],
            dev(g, image * GROUP + holder[piece]),
        )

    for d in range(SEG):
        for piece in range(2):
            if d:
                stage(d, piece).start()
                continue

            @pl.when(j == holder[piece])
            def _():
                pltpu.make_async_copy(wsend.at[piece, c], stg.at[c // 2, j], wst_r.at[c // 2]).start()

            @pl.when(j != holder[piece])
            def _():
                stage(0, piece).start()

    inputs[3].wait()
    inputs[4].wait()
    gains[c] = gain_ref[...]
    qkgs[c] = qkg_ref[...]

    def gain_copy(d):
        return remote(gain_ref, gains.at[c], g_s.at[d - 1], g_r.at[d - 1], dev((c + d) % SEG, p))

    def qkg_copy(d):
        return remote(qkg_ref, qkgs.at[c], qg_s.at[d - 1], qg_r.at[d - 1], dev((c + d) % SEG, p))

    def stale_copy(dc, dj):
        g = (c + dc) % SEG
        return remote(
            stsend.at[g], st.at[c, j], st_s.at[dc * GROUP + dj], st_r.at[c],
            dev(g, image * GROUP + (j + dj) % GROUP),
        )

    a = lax.broadcasted_iota(jnp.int32, (BLOCK, GROUP * SLOT), 0)
    b = lax.broadcasted_iota(jnp.int32, (BLOCK, GROUP * SLOT), 1)
    pick = jnp.zeros((BLOCK, GROUP * SLOT), F32)
    for slot in range(GROUP):
        hit = (a - SHARD * slot == b - SLOT * slot) & (b >= SLOT * slot) & (b < SLOT * slot + SHARD)
        pick = jnp.where(hit, 1.0, pick)
    pick = pick.astype(BF)

    def compact(half):
        pltpu.make_async_copy(stg.at[half], stg.at[half], wst_r.at[half]).wait()
        blk[half] = jnp.dot(
            pick, stg[half].reshape(GROUP * SLOT, PIECE), preferred_element_type=F32
        ).astype(BF)

    def spread(half, piece, delta):
        s = core + 2 * half
        if piece == 0:
            target = patch_of(z, (y + delta) % NY, 0)
            dst = w.at[s, 0, z, yp]
        else:
            target = patch_of((z + delta) % NZ, y, 1)
            dst = w.at[s, 1, y, z % 4]
        return remote(blk.at[half], dst, y_s.at[half, delta], y_r.at[s], dev(c, target))

    def spread_all(half, act):
        for piece in range(2):

            @pl.when(holds_a if piece == 0 else jnp.logical_not(holds_a))
            def _():
                @pl.when(core != piece)
                def _():
                    act(spread(half, piece, 0))

                for delta in (1, 7, 2, 6, 3, 5, 4):
                    act(spread(half, piece, delta))

    def spread_start(half):
        s = core + 2 * half

        @pl.when(jnp.logical_and(holds_a, core == 0))
        def _():
            pltpu.make_async_copy(blk.at[half], w.at[s, 0, z, yp], y_r.at[s]).start()

        @pl.when(jnp.logical_and(jnp.logical_not(holds_a), core == 1))
        def _():
            pltpu.make_async_copy(blk.at[half], w.at[s, 1, y, z % 4], y_r.at[s]).start()

        spread_all(half, lambda copy: copy.start())

    place = jnp.where(core == 0, z, y)

    def neighbour(step):
        nz = jnp.where(core == 0, (z + step + NZ) % NZ, z)
        ny = jnp.where(core == 0, y, (y + step + NY) % NY)
        return dev(c, patch_of(nz, ny, core))

    up, down = neighbour(1), neighbour(-1)

    def ring_block(s, t, way):
        step = 1 if (s + way) % 2 == 0 else -1
        return w.at[s, core, (place - step * t + NZ) % NZ]

    def ring(s, t, way):
        ss, rs = (rl_s, rl_r) if way == 0 else (sh_s, sh_r)
        block = ring_block(s, t, way)
        return remote(block, block, ss.at[s, t], rs.at[s, t], up if (s + way) % 2 == 0 else down)

    def to_mate(s, t, way):
        block = ring_block(s, t, way)
        index = t if way == 0 else LONG + t
        return remote(block, block, m_s.at[s, index], m_r.at[s], dev(c, mate))

    def ring_start(s):
        block = w.at[s, core, place]
        pltpu.make_async_copy(block, block, y_r.at[s]).wait()
        ring(s, 0, 0).start()
        ring(s, 0, 1).start()
        to_mate(s, 0, 0).start()

    def ring_round(s, t):
        for way, hops in ((0, LONG), (1, SHORT)):
            if t <= hops:
                block = ring_block(s, t, way)
                rs = rl_r if way == 0 else sh_r
                pltpu.make_async_copy(block, block, rs.at[s, t - 1]).wait()
                if t < hops:
                    ring(s, t, way).start()
                to_mate(s, t, way).start()

    def serve(plan):
        for s, t in plan:
            if t == 0:
                ring_start(s)
            else:
                ring_round(s, t)

    compact(0)
    spread_start(0)
    for d in range(1, SEG):
        gain_copy(d).start()
        qkg_copy(d).start()
    compact(1)

    inputs[2].wait()
    for g in range(SEG):
        for part in range(2):
            stsend[g, :, part * GW : (part + 1) * GW] = stale_ref[
                :, part * HD + g * GW : part * HD + (g + 1) * GW
            ]
    pltpu.make_async_copy(stsend.at[c], st.at[c, j], st_r.at[c]).start()
    for dj in range(GROUP):
        for dc in range(SEG):
            if dc or dj:
                stale_copy(dc, dj).start()
    inputs[5].wait()
    for g in range(SEG):
        xs[0, g] = x_ref[:, g * PIECE : (g + 1) * PIECE]

    serve([(0, 0)])
    spread_start(1)
    serve([(0, 1), (1, 0), (0, 2), (1, 1), (0, 3), (1, 2), (0, 4)])

    lane_g = lax.broadcasted_iota(jnp.int32, (1, GW), 1)
    head_of = [(lane_g >= h * HEAD) & (lane_g < (h + 1) * HEAD) for h in range(GH)]
    lane_w = lax.broadcasted_iota(jnp.int32, (1, 256), 1)
    head_in_window = [(lane_w >= 64 + h * HEAD) & (lane_w < 64 + (h + 1) * HEAD) for h in range(GH)]
    row = lax.broadcasted_iota(jnp.int32, (ROWS, IMG), 0)
    key_row = lax.broadcasted_iota(jnp.int32, (ROWS, IMG), 1)
    barred = jnp.zeros((ROWS, IMG), jnp.int32)
    live_count = live_ref[0]
    for m in range(MICRO):
        first = owner_ref[j * MICRO + m, image] * MROWS
        hit = (row >= m * MROWS) & (row < (m + 1) * MROWS) & (key_row >= first) & (key_row < first + MROWS)
        barred = jnp.where(hit, 1, barred)
    far_mask = jnp.where(barred == 1, 0.0, 1.0)
    far_mask = jnp.concatenate([far_mask] * GH, 0)
    own_r = lax.broadcasted_iota(jnp.int32, (ROWS, ROWS), 0)
    own_k = lax.broadcasted_iota(jnp.int32, (ROWS, ROWS), 1)
    own_mask = jnp.zeros((ROWS, ROWS), F32)
    for m in range(MICRO):
        lo, hi = m * MROWS, (m + 1) * MROWS
        own_mask = jnp.where((own_r >= lo) & (own_r < hi) & (own_k >= lo) & (own_k < hi), 1.0, own_mask)
    own_mask = jnp.concatenate([own_mask] * GH, 0)
    row1 = lax.broadcasted_iota(jnp.int32, (ROWS, 1), 0)
    live_rows = jnp.where(row1 < live_count * MROWS, 1.0, 0.0)
    live_rows = jnp.concatenate([live_rows] * GH, 0)

    def head_norm(part, gain_row):
        squares = part * part
        scale = jnp.zeros_like(part)
        for h in range(GH):
            mean = jnp.sum(jnp.where(head_of[h], squares, 0.0), -1, keepdims=True) * (1.0 / HEAD)
            scale = jnp.where(head_of[h], lax.rsqrt(mean + 1e-06), scale)
        return part * scale * gain_row

    def nt(lhs, rhs):
        return lax.dot_general(lhs, rhs, (((1,), (1,)), ((), ())), preferred_element_type=F32)

    def chain_front(s):
        other = 1 - core
        pltpu.make_async_copy(w.at[s, other], w.at[s, other], m_r.at[s]).wait()
        if s == 0:
            for d in range(1, SEG):
                src = (c + SEG - d) % SEG
                pltpu.make_async_copy(gain_ref, gains.at[src], g_r.at[d - 1]).wait()
                pltpu.make_async_copy(qkg_ref, qkgs.at[src], qg_r.at[d - 1]).wait()
        else:
            for d in range(1, SEG):
                src = (c + SEG - d) % SEG
                pltpu.make_async_copy(xs.at[s, src], xs.at[s, src], ag_r.at[s - 1, d - 1]).wait()
        x = jnp.concatenate([xs[s, g] for g in range(SEG)], 1).astype(F32)
        inverse = lax.rsqrt(jnp.mean(x * x, -1, keepdims=True) + 1e-06)
        normed = (x * inverse * gains[s]).astype(BF)
        qk = jnp.dot(normed, w[s, 0].reshape(D, PIECE), preferred_element_type=F32).astype(BF).astype(F32)
        w_b = jnp.concatenate(
            [w[s, 1, 2 * b + zz // 4, zz % 4] for zz in range(NZ) for b in range(NY // 2)], 0
        )
        value = jnp.dot(normed, w_b, preferred_element_type=F32).astype(BF)
        gq = qkgs[s, 0:1, :]
        gk = qkgs[s, 1:2, :]
        query = head_norm(qk[:, :GW], jnp.concatenate([gq] * GH, 1))
        key = head_norm(qk[:, GW:], jnp.concatenate([gk] * GH, 1)).astype(BF)
        query = query.astype(BF).astype(F32)
        stacked = jnp.concatenate([jnp.where(head_of[h], query, 0.0) for h in range(GH)], 0).astype(BF)
        pltpu.make_async_copy(st.at[s], st.at[s], st_r.at[s]).wait()
        kv = st[s].reshape(IMG, PIECE)
        scale = HEAD**-0.5
        far = jnp.exp(nt(stacked, kv[:, :GW]) * scale) * far_mask
        own = jnp.exp(nt(stacked, key) * scale) * own_mask
        total = jnp.sum(far, -1, keepdims=True) + jnp.sum(own, -1, keepdims=True)
        value_window = jnp.concatenate([jnp.zeros((ROWS, 64), F32), value[:, :GW].astype(F32)], 1).astype(BF)
        weighted = jnp.dot(far.astype(BF), kv[:, PIECE - 256 :], preferred_element_type=F32)
        weighted = weighted + jnp.dot(own.astype(BF), value_window, preferred_element_type=F32)
        weighted = weighted * (live_rows / total)
        attended = jnp.zeros((ROWS, 256), F32)
        for h in range(GH):
            attended = jnp.where(head_in_window[h], weighted[h * ROWS : (h + 1) * ROWS], attended)
        attended = attended.astype(BF)
        for d in (1, 2, 3, 0):
            g = (c + d) % SEG
            rows = jnp.concatenate(
                [
                    w[s, 1, 2 * b + g // 2, 2 * (g % 2) + zz, :, PIECE - 256 :]
                    for zz in range(2)
                    for b in range(NY // 2)
                ],
                0,
            )
            part = nt(attended, rows)
            if d:
                rs_out[s, d - 1] = part.astype(BF)
                rs_copy(s, d).start()
            else:
                own_part[...] = part

    def rs_copy(s, d):
        return remote(
            rs_out.at[s, d - 1], rs_in.at[s, d - 1], rs_s.at[s, d - 1], rs_r.at[s, d - 1],
            dev((c + d) % SEG, p),
        )

    def ag_copy(s, d):
        return remote(
            xs.at[s + 1, c], xs.at[s + 1, c], ag_s.at[s, d - 1], ag_r.at[s, d - 1],
            dev((c + d) % SEG, p),
        )

    def chain_back(s):
        for d in range(1, SEG):
            pltpu.make_async_copy(rs_in.at[s, d - 1], rs_in.at[s, d - 1], rs_r.at[s, d - 1]).wait()
        total = own_part[...]
        for d in range(1, SEG):
            total = total + rs_in[s, d - 1].astype(F32)
        xs[s + 1, c] = (xs[s, c].astype(F32) + total).astype(BF)
        for d in range(1, SEG):
            ag_copy(s, d).start()

    middle = [[(1, 3), (2, 0)], [(2, 3), (3, 1)], [(3, 3)], []]
    after = [[(1, 4), (2, 1), (3, 0), (2, 2)], [(2, 4), (3, 2)], [(3, 4)], []]
    for s in range(SEG):
        chain_front(s)
        serve(middle[s])
        chain_back(s)
        serve(after[s])

    for d in range(1, SEG):
        src = (c + SEG - d) % SEG
        pltpu.make_async_copy(xs.at[SEG, src], xs.at[SEG, src], ag_r.at[SEG - 1, d - 1]).wait()
    for g in range(SEG):
        out_ref[0, :, g * PIECE : (g + 1) * PIECE] = xs[c + 1, g]

    for d in range(SEG):
        for piece in range(2):
            if d:
                stage(d, piece).wait_send()
            else:

                @pl.when(j != holder[piece])
                def _():
                    stage(0, piece).wait_send()

    for d in range(1, SEG):
        gain_copy(d).wait_send()
        qkg_copy(d).wait_send()
    for dj in range(GROUP):
        for dc in range(SEG):
            if dc or dj:
                stale_copy(dc, dj).wait_send()
    for half in range(2):
        spread_all(half, lambda copy: copy.wait_send())
    for s in range(SEG):
        for way, hops in ((0, LONG), (1, SHORT)):
            for t in range(hops):
                ring(s, t, way).wait_send()
            for t in range(way, hops + 1):
                to_mate(s, t, way).wait_send()
        for d in range(1, SEG):
            rs_copy(s, d).wait_send()
            ag_copy(s, d).wait_send()


def per_device(x_in, stale_kv, owner, live, gain, qk_gain, w_qkv, w_out):
    vmem = pl.BlockSpec(memory_space=pltpu.VMEM)
    hbm = pl.BlockSpec(memory_space=pltpu.HBM)
    smem = pl.BlockSpec(memory_space=pltpu.SMEM)
    dma = pltpu.SemaphoreType.DMA
    return pl.pallas_call(
        kernel,
        out_shape=jax.ShapeDtypeStruct((1, ROWS, D), BF),
        in_specs=[hbm, hbm, smem, smem, hbm, hbm, hbm, hbm],
        out_specs=vmem,
        scratch_shapes=[
            pltpu.VMEM((ROWS, D), BF),
            pltpu.VMEM((ROWS, D), BF),
            pltpu.VMEM((1, D), F32),
            pltpu.VMEM((2, HEAD), F32),
            pltpu.VMEM((SHARD, 3 * HD), BF),
            pltpu.VMEM((SHARD, HD), BF),
            pltpu.VMEM((2, SEG, SLOT, PIECE), BF),
            pltpu.VMEM((2, GROUP, SLOT, PIECE), BF),
            pltpu.VMEM((2, BLOCK, PIECE), BF),
            pltpu.VMEM((SEG, 2, NZ, NY // 2, BLOCK, PIECE), BF),
            pltpu.VMEM((SEG, ROWS, PIECE), BF),
            pltpu.VMEM((SEG, GROUP, ROWS, PIECE), BF),
            pltpu.VMEM((SEG, 1, D), F32),
            pltpu.VMEM((SEG, 2, HEAD), F32),
            pltpu.VMEM((SEG + 1, SEG, ROWS, PIECE), BF),
            pltpu.VMEM((SEG, SEG - 1, ROWS, PIECE), BF),
            pltpu.VMEM((SEG, SEG - 1, ROWS, PIECE), BF),
            pltpu.VMEM((ROWS, PIECE), F32),
            dma((6,)), dma((SEG, 2)), dma((2,)),
            dma((SEG - 1,)), dma((SEG - 1,)), dma((SEG - 1,)), dma((SEG - 1,)),
            dma((SEG * GROUP,)), dma((SEG,)),
            dma((2, NY)), dma((SEG,)),
            dma((SEG, LONG)), dma((SEG, LONG)), dma((SEG, SHORT)), dma((SEG, SHORT)),
            dma((SEG, NZ)), dma((SEG,)),
            dma((SEG, SEG - 1)), dma((SEG, SEG - 1)), dma((SEG, SEG - 1)), dma((SEG, SEG - 1)),
        ],
        compiler_params=pltpu.CompilerParams(
            collective_id=0, has_side_effects=True, vmem_limit_bytes=62 * 2**20
        ),
    )(x_in, stale_kv[0], owner.T, live, gain, qk_gain[0], w_qkv[0], w_out[0].T)


def solution(mesh):
    in_specs = (
        P("patch", None),
        P("segment", "patch", None),
        P(),
        P("patch"),
        P("segment", None),
        P("segment", None, None),
        P("segment", "patch", None),
        P("segment", None, "patch"),
    )
    return jax.shard_map(
        per_device, mesh=mesh, in_specs=in_specs, out_specs=P("segment", "patch", None), check_vma=False
    )
```

```python
import functools

import jax
import jax.numpy as jnp
from jax import lax
from jax.experimental import pallas as pl
from jax.experimental.pallas import tpu as pltpu
from jax.sharding import PartitionSpec as P

MESH = pl.DeviceIdType.MESH
BF = jnp.bfloat16
F32 = jnp.float32

SEG = 4
NZ = 8
NY = 8
GROUP = 4
SHARD = 12
SLOT = 16
BLOCK = GROUP * SHARD
ROWS = 64
MROWS = 16
MICRO = 4
IMG = GROUP * ROWS
HEAD = 64
GH = 3
GW = GH * HEAD
PIECE = 2 * GW
D = 1536
HD = 768
LONG = NZ // 2
PARTS = (2, 1, 1, 1)
BEFORE = [(0, 0), (1, -1), (-1, 0), (0, 1), (0, 2), (1, 0), (2, -1), (0, 3), (-1, 1), (1, 1)]
MIDDLE = [[(2, 0), (3, -1), (1, 2)], [(3, 0), (2, 2)], [(3, 2)], []]
AFTER = [[(1, 3), (2, 1)], [(2, 3), (3, 1)], [(3, 3)], []]


def kernel(
    x_hbm, stale_hbm, owner_ref, live_ref, gain_hbm, qkg_hbm, wqkv_hbm, wout_hbm,
    out_ref,
    x_ref, stale_ref, gain_ref, qkg_ref, wqkv_ref, wout_ref,
    wsend, stg, blk, w, stsend, st, gains, qkgs, xs, rs_out, rs_in, own_part,
    in_sem, wst_s, wst_r, g_s, g_r, qg_s, qg_r, st_s, st_r, y_s, y_r,
    ring_s, ring_r, m_s, m_r, rs_s, rs_r, ag_s, ag_r,
):
    c = lax.axis_index("segment")
    p = lax.axis_index("patch")
    image = p // GROUP
    j = p % GROUP
    core = p % 2
    y = (p // 2) % NY
    z = p // (2 * NY)
    yp = y // 2
    zh = z // 4
    mate = p + 1 - 2 * core

    def dev(seg, patch):
        return (seg, patch)

    def patch_of(zz, yy, cc):
        return zz * (2 * NY) + yy * 2 + cc

    inputs = [
        pltpu.make_async_copy(src, dst, in_sem.at[n])
        for n, (src, dst) in enumerate(
            [
                (wqkv_hbm, wqkv_ref), (wout_hbm, wout_ref), (stale_hbm, stale_ref),
                (gain_hbm, gain_ref), (qkg_hbm, qkg_ref), (x_hbm, x_ref),
            ]
        )
    ]
    for copy in inputs:
        copy.start()

    barrier = pltpu.get_barrier_semaphore()
    partners = []
    for dc in range(SEG):
        for dj in range(GROUP):
            if dc or dj:
                partners.append(dev((c + dc) % SEG, image * GROUP + (j + dj) % GROUP))
    for dy in range(1, NY // 2):
        pair = (yp + dy) % (NY // 2)
        for low in range(4):
            partners.append(dev(c, z * (2 * NY) + pair * 4 + low))
    for dz in range(1, NZ):
        for low in range(2):
            partners.append(dev(c, patch_of((z + dz) % NZ, y, low)))
    for partner in partners:
        pl.semaphore_signal(barrier, inc=1, device_id=partner, device_id_type=MESH)

    wsend[...] = jnp.zeros_like(wsend)
    inputs[0].wait()
    inputs[1].wait()
    for g in range(SEG):
        for part in range(3):
            wsend[part // 2, g, 0:SHARD, part % 2 * GW : (part % 2 + 1) * GW] = wqkv_ref[
                :, part * HD + g * GW : part * HD + (g + 1) * GW
            ]
        wsend[1, g, 0:SHARD, GW:] = wout_ref[:, g * GW : (g + 1) * GW]
    pl.semaphore_wait(barrier, len(partners))

    def remote(src, dst, ss, rs, device):
        return pltpu.make_async_remote_copy(
            src_ref=src, dst_ref=dst, send_sem=ss, recv_sem=rs,
            device_id=device, device_id_type=MESH,
        )

    holder = [2 * (1 - zh) + c % 2, 2 * zh + c % 2]
    holds_a = y % 2 != zh

    def stage(d, piece):
        g = (c + d) % SEG
        return remote(
            wsend.at[piece, g], stg.at[c // 2, j], wst_s.at[d, piece], wst_r.at[c // 2],
            dev(g, image * GROUP + holder[piece]),
        )

    for d in range(SEG):
        for piece in range(2):
            if d:
                stage(d, piece).start()
                continue

            @pl.when(j == holder[piece])
            def _():
                pltpu.make_async_copy(wsend.at[piece, c], stg.at[c // 2, j], wst_r.at[c // 2]).start()

            @pl.when(j != holder[piece])
            def _():
                stage(0, piece).start()

    inputs[3].wait()
    inputs[4].wait()
    for g in range(SEG):
        gains[c, g] = gain_ref[:, g * PIECE : (g + 1) * PIECE]
    qkgs[c] = qkg_ref[...]

    def gain_copy(d):
        return remote(gains.at[c], gains.at[c], g_s.at[d - 1], g_r.at[d - 1], dev((c + d) % SEG, p))

    def qkg_copy(d):
        return remote(qkg_ref, qkgs.at[c], qg_s.at[d - 1], qg_r.at[d - 1], dev((c + d) % SEG, p))

    across = p + 2 - 4 * (y % 2)
    j_across = (j + 2) % GROUP

    def stale_copy(d):
        g = (c + d) % SEG
        return remote(stsend.at[g], st.at[c, j], st_s.at[d], st_r.at[0], dev(g, p))

    def stale_across():
        return remote(st.at[:, j], st.at[:, j], st_s.at[0], st_r.at[1], dev(c, across))

    def stale_mate():
        return remote(st.at[:, j], st.at[:, j], st_s.at[4], st_r.at[2], dev(c, mate))

    def stale_mate_across():
        return remote(st.at[:, j_across], st.at[:, j_across], st_s.at[5], st_r.at[3], dev(c, mate))

    def stale_wait(n, index):
        block = st.at[:, index]
        pltpu.make_async_copy(block, block, st_r.at[n]).wait()

    a = lax.broadcasted_iota(jnp.int32, (BLOCK, GROUP * SLOT), 0)
    b = lax.broadcasted_iota(jnp.int32, (BLOCK, GROUP * SLOT), 1)
    pick = jnp.zeros((BLOCK, GROUP * SLOT), F32)
    for slot in range(GROUP):
        hit = (a - SHARD * slot == b - SLOT * slot) & (b >= SLOT * slot) & (b < SLOT * slot + SHARD)
        pick = jnp.where(hit, 1.0, pick)
    pick = pick.astype(BF)

    def compact(half):
        pltpu.make_async_copy(stg.at[half], stg.at[half], wst_r.at[half]).wait()
        blk[half] = jnp.dot(
            pick, stg[half].reshape(GROUP * SLOT, PIECE), preferred_element_type=F32
        ).astype(BF)

    def spread(half, piece, delta):
        s = core + 2 * half
        if piece == 0:
            target = patch_of(z, (y + delta) % NY, 0)
            dst, slot = w.at[s, 0, z, yp], yp
        else:
            target = patch_of((z + delta) % NZ, y, 1)
            dst, slot = w.at[s, 1, y, z % 4], z % 4
        return remote(blk.at[half], dst, y_s.at[half, delta], y_r.at[s, slot], dev(c, target))

    def spread_all(s, act):
        half = s // 2
        for piece in range(2):

            @pl.when((core == s % 2) & (holds_a if piece == 0 else jnp.logical_not(holds_a)))
            def _():
                if s % 2 != piece:
                    act(spread(half, piece, 0))
                for delta in (1, 7, 2, 6, 3, 5, 4):
                    act(spread(half, piece, delta))

    def spread_start(s):
        half = s // 2
        if s % 2 == 0:

            @pl.when((core == 0) & holds_a)
            def _():
                pltpu.make_async_copy(blk.at[half], w.at[s, 0, z, yp], y_r.at[s, yp]).start()

        else:

            @pl.when((core == 1) & jnp.logical_not(holds_a))
            def _():
                pltpu.make_async_copy(blk.at[half], w.at[s, 1, y, z % 4], y_r.at[s, z % 4]).start()

        spread_all(s, lambda copy: copy.start())

    place = jnp.where(core == 0, z, y)

    def neighbour(step):
        nz = jnp.where(core == 0, (z + step + NZ) % NZ, z)
        ny = jnp.where(core == 0, y, (y + step + NY) % NY)
        return dev(c, patch_of(nz, ny, core))

    near = jnp.where(core == 0, yp, z % 4)

    def ring_block(s, way, distance, q):
        size = GROUP // PARTS[s]
        source = (place - (1 - 2 * way) * distance + NZ) % NZ
        part = (near // size + q) % PARTS[s]
        return w.at[s, core, source, pl.ds(part * size, size)], part

    def arrival_index(s, way, distance, part):
        n = 2 * (distance - 1) + (way if distance < LONG else 0)
        return (NZ - 1) * sum(PARTS[:s]) + n * PARTS[s] + part

    def ring_copy(s, way, held, step, q):
        block, part = ring_block(s, way, held, q)
        arrival = ring_r.at[arrival_index(s, way, held + step, part)]
        return remote(block, block, ring_s.at[s], arrival, neighbour((1 - 2 * way) * step))

    def ring_wait(s, way, distance, q):
        block, part = ring_block(s, way, distance, q)
        pltpu.make_async_copy(block, block, ring_r.at[arrival_index(s, way, distance, part)]).wait()

    def to_mate(s, way, distance, q):
        block, _ = ring_block(s, way, distance, q)
        return remote(block, block, m_s.at[s], m_r.at[s], dev(c, mate))

    def arrivals(s):
        return [(way, distance) for distance in range(1, LONG + 1) for way in range(2) if distance < LONG or way == s % 2]

    def ring_start(s):
        for q in range(PARTS[s]):
            block, part = ring_block(s, 0, 0, q)
            size = GROUP // PARTS[s]
            for n in range(size):
                one = w.at[s, core, place, part * size + n]
                pltpu.make_async_copy(one, one, y_r.at[s, part * size + n]).wait()
            for step in (2, 1):
                for way in range(2):
                    ring_copy(s, way, 0, step, q).start()
        for q in range(PARTS[s]):
            to_mate(s, 0, 0, q).start()

    def ring_forward(s):
        for q in range(PARTS[s]):
            for way in range(2):
                ring_wait(s, way, 2, q)
                ring_copy(s, way, 2, 1, q).start()
                if way == s % 2:
                    ring_copy(s, way, 2, 2, q).start()
        for q in range(PARTS[s]):
            for way in range(2):
                to_mate(s, way, 2, q).start()

    def ring_hand(s, distances):
        for way, distance in arrivals(s):
            if distance in distances:
                for q in range(PARTS[s]):
                    ring_wait(s, way, distance, q)
                    to_mate(s, way, distance, q).start()

    def stale_step(n):
        if n == 0:
            stale_wait(0, j)
            stale_across().start()
            stale_mate().start()
        else:
            stale_wait(1, j_across)
            stale_mate_across().start()

    def serve(plan):
        for s, t in plan:
            if s < 0:
                stale_step(t)
            elif t < 0:
                spread_start(s)
            elif t == 0:
                ring_start(s)
            elif t == 1:
                ring_forward(s)
            else:
                ring_hand(s, (1,) if t == 2 else (3, 4))

    compact(0)
    serve([(0, -1)])
    for d in range(1, SEG):
        gain_copy(d).start()
        qkg_copy(d).start()
    compact(1)

    inputs[2].wait()
    for g in range(SEG):
        for part in range(2):
            stsend[g, :, part * GW : (part + 1) * GW] = stale_ref[
                :, part * HD + g * GW : part * HD + (g + 1) * GW
            ]
    pltpu.make_async_copy(stsend.at[c], st.at[c, j], st_r.at[0]).start()
    for d in range(1, SEG):
        stale_copy(d).start()
    inputs[5].wait()
    for g in range(SEG):
        xs[0, g] = x_ref[:, g * PIECE : (g + 1) * PIECE]

    serve(BEFORE)

    lane_g = lax.broadcasted_iota(jnp.int32, (1, GW), 1)
    head_of = [(lane_g >= h * HEAD) & (lane_g < (h + 1) * HEAD) for h in range(GH)]
    lane_w = lax.broadcasted_iota(jnp.int32, (1, 256), 1)
    head_in_window = [(lane_w >= 64 + h * HEAD) & (lane_w < 64 + (h + 1) * HEAD) for h in range(GH)]
    row = lax.broadcasted_iota(jnp.int32, (ROWS, IMG), 0)
    key_row = lax.broadcasted_iota(jnp.int32, (ROWS, IMG), 1)
    barred = jnp.zeros((ROWS, IMG), jnp.int32)
    live_count = live_ref[0]
    for m in range(MICRO):
        first = owner_ref[j * MICRO + m, image] * MROWS
        hit = (row >= m * MROWS) & (row < (m + 1) * MROWS) & (key_row >= first) & (key_row < first + MROWS)
        barred = jnp.where(hit, 1, barred)
    far_mask = jnp.where(barred == 1, 0.0, 1.0)
    far_mask = jnp.concatenate([far_mask] * GH, 0)
    own_r = lax.broadcasted_iota(jnp.int32, (ROWS, ROWS), 0)
    own_k = lax.broadcasted_iota(jnp.int32, (ROWS, ROWS), 1)
    own_mask = jnp.zeros((ROWS, ROWS), F32)
    for m in range(MICRO):
        lo, hi = m * MROWS, (m + 1) * MROWS
        own_mask = jnp.where((own_r >= lo) & (own_r < hi) & (own_k >= lo) & (own_k < hi), 1.0, own_mask)
    own_mask = jnp.concatenate([own_mask] * GH, 0)
    row1 = lax.broadcasted_iota(jnp.int32, (ROWS, 1), 0)
    live_rows = jnp.where(row1 < live_count * MROWS, 1.0, 0.0)
    live_rows = jnp.concatenate([live_rows] * GH, 0)

    def head_norm(part, gain_row):
        squares = part * part
        scale = jnp.zeros_like(part)
        for h in range(GH):
            mean = jnp.sum(jnp.where(head_of[h], squares, 0.0), -1, keepdims=True) * (1.0 / HEAD)
            scale = jnp.where(head_of[h], lax.rsqrt(mean + 1e-06), scale)
        return part * scale * gain_row

    def nt(lhs, rhs):
        return lax.dot_general(lhs, rhs, (((1,), (1,)), ((), ())), preferred_element_type=F32)

    def w_b_rows(s, g):
        return jnp.concatenate(
            [w[s, 1, 2 * b + g // 2, 2 * (g % 2) + zz] for zz in range(2) for b in range(NY // 2)], 0
        )

    def chain_front(s):
        other = 1 - core
        pltpu.make_async_copy(w.at[s, other], w.at[s, other], m_r.at[s]).wait()
        if s == 0:
            for d in range(1, SEG):
                src = (c + SEG - d) % SEG
                pltpu.make_async_copy(gains.at[src], gains.at[src], g_r.at[d - 1]).wait()
                pltpu.make_async_copy(qkg_ref, qkgs.at[src], qg_r.at[d - 1]).wait()
        product_a = jnp.zeros((ROWS, PIECE), F32)
        product_b = jnp.zeros((ROWS, PIECE), F32)
        squares = jnp.zeros((ROWS, 1), F32)
        for d in (0, 1, 3, 2):
            g = (c + SEG - d) % SEG
            if s and d:
                pltpu.make_async_copy(xs.at[s, g], xs.at[s, g], ag_r.at[s - 1, d - 1]).wait()
            x = xs[s, g].astype(F32)
            squares = squares + jnp.sum(x * x, -1, keepdims=True)
            scaled = (x * gains[s, g]).astype(BF)
            w_a = w[s, 0, pl.ds(2 * g, 2)].reshape(PIECE, PIECE)
            product_a = product_a + jnp.dot(scaled, w_a, preferred_element_type=F32)
            product_b = product_b + jnp.dot(scaled, w_b_rows(s, g), preferred_element_type=F32)
        inverse = lax.rsqrt(squares * (1.0 / D) + 1e-06)
        qk = (product_a * inverse).astype(BF).astype(F32)
        value = (product_b * inverse).astype(BF)
        gq = qkgs[s, 0:1, :]
        gk = qkgs[s, 1:2, :]
        query = head_norm(qk[:, :GW], jnp.concatenate([gq] * GH, 1))
        key = head_norm(qk[:, GW:], jnp.concatenate([gk] * GH, 1)).astype(BF)
        query = query.astype(BF).astype(F32)
        stacked = jnp.concatenate([jnp.where(head_of[h], query, 0.0) for h in range(GH)], 0).astype(BF)
        if s == 0:
            stale_wait(2, j + 1 - 2 * core)
            stale_wait(3, j_across + 1 - 2 * core)
        kv = st[s].reshape(IMG, PIECE)
        scale = HEAD**-0.5
        far = jnp.exp(nt(stacked, kv[:, :GW]) * scale) * far_mask
        own = jnp.exp(nt(stacked, key) * scale) * own_mask
        total = jnp.sum(far, -1, keepdims=True) + jnp.sum(own, -1, keepdims=True)
        value_window = jnp.concatenate([jnp.zeros((ROWS, 64), F32), value[:, :GW].astype(F32)], 1).astype(BF)
        weighted = jnp.dot(far.astype(BF), kv[:, PIECE - 256 :], preferred_element_type=F32)
        weighted = weighted + jnp.dot(own.astype(BF), value_window, preferred_element_type=F32)
        weighted = weighted * (live_rows / total)
        attended = jnp.zeros((ROWS, 256), F32)
        for h in range(GH):
            attended = jnp.where(head_in_window[h], weighted[h * ROWS : (h + 1) * ROWS], attended)
        attended = attended.astype(BF)
        for d in (2, 1, 3, 0):
            g = (c + d) % SEG
            part = nt(attended, w_b_rows(s, g)[:, PIECE - 256 :])
            if d:
                rs_out[s, d - 1] = part.astype(BF)
                rs_copy(s, d).start()
            else:
                own_part[...] = part

    def rs_copy(s, d):
        return remote(
            rs_out.at[s, d - 1], rs_in.at[s, d - 1], rs_s.at[s], rs_r.at[s],
            dev((c + d) % SEG, p),
        )

    def ag_copy(s, d):
        return remote(
            xs.at[s + 1, c], xs.at[s + 1, c], ag_s.at[s], ag_r.at[s, d - 1],
            dev((c + d) % SEG, p),
        )

    def chain_back(s):
        pltpu.make_async_copy(rs_in.at[s], rs_in.at[s], rs_r.at[s]).wait()
        total = own_part[...]
        for d in range(1, SEG):
            total = total + rs_in[s, d - 1].astype(F32)
        xs[s + 1, c] = (xs[s, c].astype(F32) + total).astype(BF)
        for d in range(1, SEG):
            ag_copy(s, d).start()

    for s in range(SEG):
        chain_front(s)
        serve(MIDDLE[s])
        chain_back(s)
        serve(AFTER[s])

    for d in range(1, SEG):
        src = (c + SEG - d) % SEG
        pltpu.make_async_copy(xs.at[SEG, src], xs.at[SEG, src], ag_r.at[SEG - 1, d - 1]).wait()
    for g in range(SEG):
        out_ref[0, :, g * PIECE : (g + 1) * PIECE] = xs[c + 1, g]

    for d in range(SEG):
        for piece in range(2):
            if d:
                stage(d, piece).wait_send()
            else:

                @pl.when(j != holder[piece])
                def _():
                    stage(0, piece).wait_send()

    for d in range(1, SEG):
        gain_copy(d).wait_send()
        qkg_copy(d).wait_send()
        stale_copy(d).wait_send()
    stale_across().wait_send()
    stale_mate().wait_send()
    stale_mate_across().wait_send()
    for s in range(SEG):
        spread_all(s, lambda copy: copy.wait_send())
    for s in range(SEG):
        for block, sem in (
            (w.at[s, core, pl.ds(0, NZ - 1)], ring_s), (w.at[s, core], m_s), (rs_out.at[s], rs_s), (rs_out.at[s], ag_s)
        ):
            pltpu.make_async_copy(block, block, sem.at[s]).wait()


def per_device(x_in, stale_kv, owner, live, gain, qk_gain, w_qkv, w_out):
    vmem = pl.BlockSpec(memory_space=pltpu.VMEM)
    hbm = pl.BlockSpec(memory_space=pltpu.HBM)
    smem = pl.BlockSpec(memory_space=pltpu.SMEM)
    dma = pltpu.SemaphoreType.DMA
    return pl.pallas_call(
        kernel,
        out_shape=jax.ShapeDtypeStruct((1, ROWS, D), BF),
        in_specs=[hbm, hbm, smem, smem, hbm, hbm, hbm, hbm],
        out_specs=vmem,
        scratch_shapes=[
            pltpu.VMEM((ROWS, D), BF),
            pltpu.VMEM((ROWS, D), BF),
            pltpu.VMEM((1, D), F32),
            pltpu.VMEM((2, HEAD), F32),
            pltpu.VMEM((SHARD, 3 * HD), BF),
            pltpu.VMEM((SHARD, HD), BF),
            pltpu.VMEM((2, SEG, SLOT, PIECE), BF),
            pltpu.VMEM((2, GROUP, SLOT, PIECE), BF),
            pltpu.VMEM((2, BLOCK, PIECE), BF),
            pltpu.VMEM((SEG, 2, NZ, NY // 2, BLOCK, PIECE), BF),
            pltpu.VMEM((SEG, ROWS, PIECE), BF),
            pltpu.VMEM((SEG, GROUP, ROWS, PIECE), BF),
            pltpu.VMEM((SEG, SEG, 1, PIECE), F32),
            pltpu.VMEM((SEG, 2, HEAD), F32),
            pltpu.VMEM((SEG + 1, SEG, ROWS, PIECE), BF),
            pltpu.VMEM((SEG, SEG - 1, ROWS, PIECE), BF),
            pltpu.VMEM((SEG, SEG - 1, ROWS, PIECE), BF),
            pltpu.VMEM((ROWS, PIECE), F32),
            dma((6,)), dma((SEG, 2)), dma((2,)),
            dma((SEG - 1,)), dma((SEG - 1,)), dma((SEG - 1,)), dma((SEG - 1,)),
            dma((6,)), dma((SEG,)),
            dma((2, NY)), dma((SEG, GROUP)),
            dma((SEG,)), dma(((NZ - 1) * sum(PARTS),)), dma((SEG,)), dma((SEG,)),
            dma((SEG,)), dma((SEG,)), dma((SEG,)), dma((SEG, SEG - 1)),
        ],
        compiler_params=pltpu.CompilerParams(
            collective_id=0, has_side_effects=True, vmem_limit_bytes=62 * 2**20
        ),
    )(x_in, stale_kv[0], owner.T, live, gain, qk_gain[0], w_qkv[0], w_out[0].T)


def solution(mesh):
    in_specs = (
        P("patch", None),
        P("segment", "patch", None),
        P(),
        P("patch"),
        P("segment", None),
        P("segment", None, None),
        P("segment", "patch", None),
        P("segment", None, "patch"),
    )
    return jax.shard_map(
        per_device, mesh=mesh, in_specs=in_specs, out_specs=P("segment", "patch", None), check_vma=False
    )
```

```python
import functools

import jax
import jax.numpy as jnp
from jax import lax
from jax.experimental import pallas as pl
from jax.experimental.pallas import tpu as pltpu
from jax.sharding import PartitionSpec as P

MESH = pl.DeviceIdType.MESH
BF = jnp.bfloat16
F32 = jnp.float32

SEG = 4
NZ = 8
NY = 8
GROUP = 4
SHARD = 12
SLOT = 16
BLOCK = GROUP * SHARD
ROWS = 64
MROWS = 16
MICRO = 4
IMG = GROUP * ROWS
HEAD = 64
GH = 3
GW = GH * HEAD
PIECE = 2 * GW
D = 1536
HD = 768
LONG = NZ // 2
PARTS = (2, 1, 1, 1)
FIRST = [(0, -1), (1, -1)]
BEFORE = [(0, 0), (-1, 0), (0, 1), (0, 2), (1, 0), (2, -1), (0, 3), (-1, 1), (1, 1)]
MIDDLE = [[(-1, 2), (2, 0), (3, -1), (1, 2)], [(3, 0), (2, 2)], [(3, 2)], []]
AFTER = [[(-1, 3), (1, 3), (2, 1)], [(2, 3), (3, 1)], [(3, 3)], []]


def kernel(
    x_hbm, stale_hbm, owner_ref, live_ref, gain_hbm, qkg_hbm, wqkv_hbm, wout_hbm,
    out_ref,
    x_ref, stale_ref, gain_ref, qkg_ref, wqkv_ref, wout_ref,
    wsend, stg, blk, w, stsend, st, gains, qkgs, xs, rs_out, rs_in, own_part,
    in_sem, wst_s, wst_r, g_s, g_r, qg_s, qg_r, st_s, st_r, y_s, y_r,
    ring_s, ring_r, m_s, m_r, rs_s, rs_r, ag_s, ag_r,
):
    c = lax.axis_index("segment")
    p = lax.axis_index("patch")
    image = p // GROUP
    j = p % GROUP
    core = p % 2
    y = (p // 2) % NY
    z = p // (2 * NY)
    yp = y // 2
    zh = z // 4
    mate = p + 1 - 2 * core

    def dev(seg, patch):
        return (seg, patch)

    def patch_of(zz, yy, cc):
        return zz * (2 * NY) + yy * 2 + cc

    inputs = [
        pltpu.make_async_copy(src, dst, in_sem.at[n])
        for n, (src, dst) in enumerate(
            [
                (wqkv_hbm, wqkv_ref), (wout_hbm, wout_ref), (stale_hbm, stale_ref),
                (gain_hbm, gain_ref), (qkg_hbm, qkg_ref), (x_hbm, x_ref),
            ]
        )
    ]
    for copy in inputs:
        copy.start()

    barrier = pltpu.get_barrier_semaphore()
    partners = []
    for dc in range(SEG):
        for dj in range(GROUP):
            if dc or dj:
                partners.append(dev((c + dc) % SEG, image * GROUP + (j + dj) % GROUP))
    for dy in range(1, NY // 2):
        pair = (yp + dy) % (NY // 2)
        for low in range(4):
            partners.append(dev(c, z * (2 * NY) + pair * 4 + low))
    for dz in range(1, NZ):
        for low in range(2):
            partners.append(dev(c, patch_of((z + dz) % NZ, y, low)))
    for partner in partners:
        pl.semaphore_signal(barrier, inc=1, device_id=partner, device_id_type=MESH)

    wsend[...] = jnp.zeros_like(wsend)
    inputs[0].wait()
    inputs[1].wait()
    for g in range(SEG):
        for part in range(3):
            wsend[part // 2, g, 0:SHARD, part % 2 * GW : (part % 2 + 1) * GW] = wqkv_ref[
                :, part * HD + g * GW : part * HD + (g + 1) * GW
            ]
        wsend[1, g, 0:SHARD, GW:] = wout_ref[:, g * GW : (g + 1) * GW]
    pl.semaphore_wait(barrier, len(partners))

    def remote(src, dst, ss, rs, device):
        return pltpu.make_async_remote_copy(
            src_ref=src, dst_ref=dst, send_sem=ss, recv_sem=rs,
            device_id=device, device_id_type=MESH,
        )

    holder = [2 * (1 - zh) + c % 2, 2 * zh + c % 2]
    holds_a = y % 2 != zh

    def stage(d, piece):
        g = (c + d) % SEG
        return remote(
            wsend.at[piece, g], stg.at[c // 2, j], wst_s.at[d, piece], wst_r.at[c // 2],
            dev(g, image * GROUP + holder[piece]),
        )

    for d in (2, 1, 3, 0):
        for piece in range(2):
            if d:
                stage(d, piece).start()
                continue

            @pl.when(j == holder[piece])
            def _():
                pltpu.make_async_copy(wsend.at[piece, c], stg.at[c // 2, j], wst_r.at[c // 2]).start()

            @pl.when(j != holder[piece])
            def _():
                stage(0, piece).start()

    inputs[3].wait()
    inputs[4].wait()
    for g in range(SEG):
        gains[c, g] = gain_ref[:, g * PIECE : (g + 1) * PIECE]
    qkgs[c] = qkg_ref[...]

    def gain_copy(d):
        return remote(gains.at[c], gains.at[c], g_s.at[d - 1], g_r.at[d - 1], dev((c + d) % SEG, p))

    def qkg_copy(d):
        return remote(qkg_ref, qkgs.at[c], qg_s.at[d - 1], qg_r.at[d - 1], dev((c + d) % SEG, p))

    across = p + 2 - 4 * (y % 2)
    j_across = (j + 2) % GROUP

    def stale_copy(d):
        g = (c + d) % SEG
        return remote(stsend.at[g], st.at[c, j], st_s.at[d], st_r.at[0], dev(g, p))

    def stale_rows(rest, index):
        return st.at[pl.ds(1, SEG - 1), index] if rest else st.at[0, index]

    def stale_across(rest):
        block = stale_rows(rest, j)
        return remote(block, block, st_s.at[4 + rest], st_r.at[1 + rest], dev(c, across))

    def stale_mate(rest):
        block = stale_rows(rest, j)
        return remote(block, block, st_s.at[6 + rest], st_r.at[3 + rest], dev(c, mate))

    def stale_mate_across(rest):
        block = stale_rows(rest, j_across)
        return remote(block, block, st_s.at[8 + rest], st_r.at[5 + rest], dev(c, mate))

    def stale_wait(block, n):
        pltpu.make_async_copy(block, block, st_r.at[n]).wait()

    a = lax.broadcasted_iota(jnp.int32, (BLOCK, GROUP * SLOT), 0)
    b = lax.broadcasted_iota(jnp.int32, (BLOCK, GROUP * SLOT), 1)
    pick = jnp.zeros((BLOCK, GROUP * SLOT), F32)
    for slot in range(GROUP):
        hit = (a - SHARD * slot == b - SLOT * slot) & (b >= SLOT * slot) & (b < SLOT * slot + SHARD)
        pick = jnp.where(hit, 1.0, pick)
    pick = pick.astype(BF)

    def compact(half):
        pltpu.make_async_copy(stg.at[half], stg.at[half], wst_r.at[half]).wait()
        blk[half] = jnp.dot(
            pick, stg[half].reshape(GROUP * SLOT, PIECE), preferred_element_type=F32
        ).astype(BF)

    def spread(half, piece, delta):
        s = core + 2 * half
        if piece == 0:
            target = patch_of(z, (y + delta) % NY, 0)
            dst, slot = w.at[s, 0, z, yp], yp
        else:
            target = patch_of((z + delta) % NZ, y, 1)
            dst, slot = w.at[s, 1, y, z % 4], z % 4
        return remote(blk.at[half], dst, y_s.at[half, delta], y_r.at[s, slot // 2], dev(c, target))

    def spread_all(s, act):
        half = s // 2
        for piece in range(2):

            @pl.when((core == s % 2) & (holds_a if piece == 0 else jnp.logical_not(holds_a)))
            def _():
                if s % 2 != piece:
                    act(spread(half, piece, 0))
                for delta in (4, 3, 5, 2, 6, 1, 7):
                    act(spread(half, piece, delta))

    def spread_start(s):
        half = s // 2
        if s % 2 == 0:

            @pl.when((core == 0) & holds_a)
            def _():
                pltpu.make_async_copy(blk.at[half], w.at[s, 0, z, yp], y_r.at[s, yp // 2]).start()

        else:

            @pl.when((core == 1) & jnp.logical_not(holds_a))
            def _():
                pltpu.make_async_copy(blk.at[half], w.at[s, 1, y, z % 4], y_r.at[s, z % 4 // 2]).start()

        spread_all(s, lambda copy: copy.start())

    place = jnp.where(core == 0, z, y)

    def neighbour(step):
        nz = jnp.where(core == 0, (z + step + NZ) % NZ, z)
        ny = jnp.where(core == 0, y, (y + step + NY) % NY)
        return dev(c, patch_of(nz, ny, core))

    near = jnp.where(core == 0, yp, z % 4)

    def ring_block(s, way, distance, q):
        size = GROUP // PARTS[s]
        source = (place - (1 - 2 * way) * distance + NZ) % NZ
        part = (near // size + q) % PARTS[s]
        return w.at[s, core, source, pl.ds(part * size, size)], part

    def arrival_index(s, way, distance, part):
        n = 2 * (distance - 1) + (way if distance < LONG else 0)
        return (NZ - 1) * sum(PARTS[:s]) + n * PARTS[s] + part

    def ring_copy(s, way, held, step, q):
        block, part = ring_block(s, way, held, q)
        arrival = ring_r.at[arrival_index(s, way, held + step, part)]
        return remote(block, block, ring_s.at[s], arrival, neighbour((1 - 2 * way) * step))

    def ring_wait(s, way, distance, q):
        block, part = ring_block(s, way, distance, q)
        pltpu.make_async_copy(block, block, ring_r.at[arrival_index(s, way, distance, part)]).wait()

    def to_mate(s, way, distance, q):
        block, _ = ring_block(s, way, distance, q)
        return remote(block, block, m_s.at[s], m_r.at[s], dev(c, mate))

    def arrivals(s):
        return [(way, distance) for distance in range(1, LONG + 1) for way in range(2) if distance < LONG or way == s % 2]

    def ring_start(s):
        for q in range(PARTS[s]):
            block, part = ring_block(s, 0, 0, q)
            size = GROUP // PARTS[s]
            for n in range(size // 2):
                half = part * size // 2 + n
                two = w.at[s, core, place, pl.ds(2 * half, 2)]
                pltpu.make_async_copy(two, two, y_r.at[s, half]).wait()
            for step in (2, 1):
                for way in range(2):
                    ring_copy(s, way, 0, step, q).start()
        for q in range(PARTS[s]):
            to_mate(s, 0, 0, q).start()

    def ring_forward(s):
        for q in range(PARTS[s]):
            for way in range(2):
                ring_wait(s, way, 2, q)
                if way == s % 2:
                    ring_copy(s, way, 2, 2, q).start()
                ring_copy(s, way, 2, 1, q).start()
        for q in range(PARTS[s]):
            for way in range(2):
                to_mate(s, way, 2, q).start()

    def ring_hand(s, distances):
        for way, distance in arrivals(s):
            if distance in distances:
                for q in range(PARTS[s]):
                    ring_wait(s, way, distance, q)
                    to_mate(s, way, distance, q).start()

    def stale_step(n):
        rest = n // 2
        if n % 2 == 0:
            if rest == 0:
                stale_wait(st.at[:, j], 0)
            stale_across(rest).start()
            stale_mate(rest).start()
        else:
            stale_wait(stale_rows(rest, j_across), 1 + rest)
            stale_mate_across(rest).start()

    def serve(plan):
        for s, t in plan:
            if s < 0:
                stale_step(t)
            elif t < 0:
                spread_start(s)
            elif t == 0:
                ring_start(s)
            elif t == 1:
                ring_forward(s)
            else:
                ring_hand(s, (1,) if t == 2 else (3, 4))

    compact(0)
    serve(FIRST)
    for d in range(1, SEG):
        gain_copy(d).start()
        qkg_copy(d).start()
    compact(1)

    inputs[2].wait()
    for g in range(SEG):
        for part in range(2):
            stsend[g, :, part * GW : (part + 1) * GW] = stale_ref[
                :, part * HD + g * GW : part * HD + (g + 1) * GW
            ]
    pltpu.make_async_copy(stsend.at[c], st.at[c, j], st_r.at[0]).start()
    for d in range(1, SEG):
        stale_copy(d).start()
    inputs[5].wait()
    for g in range(SEG):
        xs[0, g] = x_ref[:, g * PIECE : (g + 1) * PIECE]

    serve(BEFORE)

    lane_g = lax.broadcasted_iota(jnp.int32, (1, GW), 1)
    head_of = [(lane_g >= h * HEAD) & (lane_g < (h + 1) * HEAD) for h in range(GH)]
    lane_w = lax.broadcasted_iota(jnp.int32, (1, 256), 1)
    head_in_window = [(lane_w >= 64 + h * HEAD) & (lane_w < 64 + (h + 1) * HEAD) for h in range(GH)]
    row = lax.broadcasted_iota(jnp.int32, (ROWS, IMG), 0)
    key_row = lax.broadcasted_iota(jnp.int32, (ROWS, IMG), 1)
    barred = jnp.zeros((ROWS, IMG), jnp.int32)
    live_count = live_ref[0]
    for m in range(MICRO):
        first = owner_ref[j * MICRO + m, image] * MROWS
        hit = (row >= m * MROWS) & (row < (m + 1) * MROWS) & (key_row >= first) & (key_row < first + MROWS)
        barred = jnp.where(hit, 1, barred)
    far_mask = jnp.where(barred == 1, 0.0, 1.0)
    far_mask = jnp.concatenate([far_mask] * GH, 0)
    own_r = lax.broadcasted_iota(jnp.int32, (ROWS, ROWS), 0)
    own_k = lax.broadcasted_iota(jnp.int32, (ROWS, ROWS), 1)
    own_mask = jnp.zeros((ROWS, ROWS), F32)
    for m in range(MICRO):
        lo, hi = m * MROWS, (m + 1) * MROWS
        own_mask = jnp.where((own_r >= lo) & (own_r < hi) & (own_k >= lo) & (own_k < hi), 1.0, own_mask)
    own_mask = jnp.concatenate([own_mask] * GH, 0)
    row1 = lax.broadcasted_iota(jnp.int32, (ROWS, 1), 0)
    live_rows = jnp.where(row1 < live_count * MROWS, 1.0, 0.0)
    live_rows = jnp.concatenate([live_rows] * GH, 0)

    def head_norm(part, gain_row):
        squares = part * part
        scale = jnp.zeros_like(part)
        for h in range(GH):
            mean = jnp.sum(jnp.where(head_of[h], squares, 0.0), -1, keepdims=True) * (1.0 / HEAD)
            scale = jnp.where(head_of[h], lax.rsqrt(mean + 1e-06), scale)
        return part * scale * gain_row

    def nt(lhs, rhs):
        return lax.dot_general(lhs, rhs, (((1,), (1,)), ((), ())), preferred_element_type=F32)

    def w_b_rows(s, g):
        return jnp.concatenate(
            [w[s, 1, 2 * b + g // 2, 2 * (g % 2) + zz] for zz in range(2) for b in range(NY // 2)], 0
        )

    def chain_front(s):
        other = 1 - core
        pltpu.make_async_copy(w.at[s, other], w.at[s, other], m_r.at[s]).wait()
        if s == 0:
            for d in range(1, SEG):
                src = (c + SEG - d) % SEG
                pltpu.make_async_copy(gains.at[src], gains.at[src], g_r.at[d - 1]).wait()
                pltpu.make_async_copy(qkg_ref, qkgs.at[src], qg_r.at[d - 1]).wait()
        product_a = jnp.zeros((ROWS, PIECE), F32)
        product_b = jnp.zeros((ROWS, PIECE), F32)
        squares = jnp.zeros((ROWS, 1), F32)
        for d in (0, 1, 3, 2):
            g = (c + SEG - d) % SEG
            if s and d:
                pltpu.make_async_copy(xs.at[s, g], xs.at[s, g], ag_r.at[s - 1, d - 1]).wait()
            x = xs[s, g].astype(F32)
            squares = squares + jnp.sum(x * x, -1, keepdims=True)
            scaled = (x * gains[s, g]).astype(BF)
            w_a = w[s, 0, pl.ds(2 * g, 2)].reshape(PIECE, PIECE)
            product_a = product_a + jnp.dot(scaled, w_a, preferred_element_type=F32)
            product_b = product_b + jnp.dot(scaled, w_b_rows(s, g), preferred_element_type=F32)
        inverse = lax.rsqrt(squares * (1.0 / D) + 1e-06)
        qk = (product_a * inverse).astype(BF).astype(F32)
        value = (product_b * inverse).astype(BF)
        gq = qkgs[s, 0:1, :]
        gk = qkgs[s, 1:2, :]
        query = head_norm(qk[:, :GW], jnp.concatenate([gq] * GH, 1))
        key = head_norm(qk[:, GW:], jnp.concatenate([gk] * GH, 1)).astype(BF)
        query = query.astype(BF).astype(F32)
        stacked = jnp.concatenate([jnp.where(head_of[h], query, 0.0) for h in range(GH)], 0).astype(BF)
        if s < 2:
            stale_wait(stale_rows(s, j + 1 - 2 * core), 3 + s)
            stale_wait(stale_rows(s, j_across + 1 - 2 * core), 5 + s)
        kv = st[s].reshape(IMG, PIECE)
        scale = HEAD**-0.5
        far = jnp.exp(nt(stacked, kv[:, :GW]) * scale) * far_mask
        own = jnp.exp(nt(stacked, key) * scale) * own_mask
        total = jnp.sum(far, -1, keepdims=True) + jnp.sum(own, -1, keepdims=True)
        value_window = jnp.concatenate([jnp.zeros((ROWS, 64), F32), value[:, :GW].astype(F32)], 1).astype(BF)
        weighted = jnp.dot(far.astype(BF), kv[:, PIECE - 256 :], preferred_element_type=F32)
        weighted = weighted + jnp.dot(own.astype(BF), value_window, preferred_element_type=F32)
        weighted = weighted * (live_rows / total)
        attended = jnp.zeros((ROWS, 256), F32)
        for h in range(GH):
            attended = jnp.where(head_in_window[h], weighted[h * ROWS : (h + 1) * ROWS], attended)
        attended = attended.astype(BF)
        for d in (2, 1, 3, 0):
            g = (c + d) % SEG
            part = nt(attended, w_b_rows(s, g)[:, PIECE - 256 :])
            if d:
                rs_out[s, d - 1] = part.astype(BF)
                rs_copy(s, d).start()
            else:
                own_part[...] = part

    def rs_copy(s, d):
        return remote(
            rs_out.at[s, d - 1], rs_in.at[s, d - 1], rs_s.at[s], rs_r.at[s],
            dev((c + d) % SEG, p),
        )

    def ag_copy(s, d):
        return remote(
            xs.at[s + 1, c], xs.at[s + 1, c], ag_s.at[s], ag_r.at[s, d - 1],
            dev((c + d) % SEG, p),
        )

    def last_copy():
        return remote(
            xs.at[SEG, c], xs.at[SEG, c], ag_s.at[SEG - 1], ag_r.at[SEG - 1, (2 * SEG - 2 - c) % SEG],
            dev(SEG - 1, p),
        )

    def chain_back(s):
        pltpu.make_async_copy(rs_in.at[s], rs_in.at[s], rs_r.at[s]).wait()
        total = own_part[...]
        for d in range(1, SEG):
            total = total + rs_in[s, d - 1].astype(F32)
        xs[s + 1, c] = (xs[s, c].astype(F32) + total).astype(BF)
        if s + 1 < SEG:
            for d in (2, 1, 3):
                ag_copy(s, d).start()
        else:

            @pl.when(c != SEG - 1)
            def _():
                last_copy().start()

    for s in range(SEG):
        chain_front(s)
        serve(MIDDLE[s])
        chain_back(s)
        serve(AFTER[s])

    @pl.when(c == SEG - 1)
    def _():
        for d in range(1, SEG):
            src = (c + SEG - d) % SEG
            pltpu.make_async_copy(xs.at[SEG, src], xs.at[SEG, src], ag_r.at[SEG - 1, d - 1]).wait()

    for g in range(SEG):
        out_ref[0, :, g * PIECE : (g + 1) * PIECE] = xs[c + 1, g]

    for d in range(SEG):
        for piece in range(2):
            if d:
                stage(d, piece).wait_send()
            else:

                @pl.when(j != holder[piece])
                def _():
                    stage(0, piece).wait_send()

    for d in range(1, SEG):
        gain_copy(d).wait_send()
        qkg_copy(d).wait_send()
        stale_copy(d).wait_send()
    for rest in range(2):
        stale_across(rest).wait_send()
        stale_mate(rest).wait_send()
        stale_mate_across(rest).wait_send()
    for s in range(SEG):
        spread_all(s, lambda copy: copy.wait_send())
    for s in range(SEG):
        for block, sem in (
            (w.at[s, core, pl.ds(0, NZ - 1)], ring_s), (w.at[s, core], m_s), (rs_out.at[s], rs_s), (rs_out.at[s], ag_s)
        ):
            if sem is not ag_s or s + 1 < SEG:
                pltpu.make_async_copy(block, block, sem.at[s]).wait()

    @pl.when(c != SEG - 1)
    def _():
        last_copy().wait_send()


def per_device(x_in, stale_kv, owner, live, gain, qk_gain, w_qkv, w_out):
    vmem = pl.BlockSpec(memory_space=pltpu.VMEM)
    hbm = pl.BlockSpec(memory_space=pltpu.HBM)
    smem = pl.BlockSpec(memory_space=pltpu.SMEM)
    dma = pltpu.SemaphoreType.DMA
    return pl.pallas_call(
        kernel,
        out_shape=jax.ShapeDtypeStruct((1, ROWS, D), BF),
        in_specs=[hbm, hbm, smem, smem, hbm, hbm, hbm, hbm],
        out_specs=vmem,
        scratch_shapes=[
            pltpu.VMEM((ROWS, D), BF),
            pltpu.VMEM((ROWS, D), BF),
            pltpu.VMEM((1, D), F32),
            pltpu.VMEM((2, HEAD), F32),
            pltpu.VMEM((SHARD, 3 * HD), BF),
            pltpu.VMEM((SHARD, HD), BF),
            pltpu.VMEM((2, SEG, SLOT, PIECE), BF),
            pltpu.VMEM((2, GROUP, SLOT, PIECE), BF),
            pltpu.VMEM((2, BLOCK, PIECE), BF),
            pltpu.VMEM((SEG, 2, NZ, NY // 2, BLOCK, PIECE), BF),
            pltpu.VMEM((SEG, ROWS, PIECE), BF),
            pltpu.VMEM((SEG, GROUP, ROWS, PIECE), BF),
            pltpu.VMEM((SEG, SEG, 1, PIECE), F32),
            pltpu.VMEM((SEG, 2, HEAD), F32),
            pltpu.VMEM((SEG + 1, SEG, ROWS, PIECE), BF),
            pltpu.VMEM((SEG, SEG - 1, ROWS, PIECE), BF),
            pltpu.VMEM((SEG, SEG - 1, ROWS, PIECE), BF),
            pltpu.VMEM((ROWS, PIECE), F32),
            dma((6,)), dma((SEG, 2)), dma((2,)),
            dma((SEG - 1,)), dma((SEG - 1,)), dma((SEG - 1,)), dma((SEG - 1,)),
            dma((10,)), dma((7,)),
            dma((2, NY)), dma((SEG, 2)),
            dma((SEG,)), dma(((NZ - 1) * sum(PARTS),)), dma((SEG,)), dma((SEG,)),
            dma((SEG,)), dma((SEG,)), dma((SEG,)), dma((SEG, SEG - 1)),
        ],
        compiler_params=pltpu.CompilerParams(
            collective_id=0, has_side_effects=True, vmem_limit_bytes=62 * 2**20
        ),
    )(x_in, stale_kv[0], owner.T, live, gain, qk_gain[0], w_qkv[0], w_out[0].T)


def solution(mesh):
    in_specs = (
        P("patch", None),
        P("segment", "patch", None),
        P(),
        P("patch"),
        P("segment", None),
        P("segment", None, None),
        P("segment", "patch", None),
        P("segment", None, "patch"),
    )
    return jax.shard_map(
        per_device, mesh=mesh, in_specs=in_specs, out_specs=P("segment", "patch", None), check_vma=False
    )
```

```python
import functools

import jax
import jax.numpy as jnp
from jax import lax
from jax.experimental import pallas as pl
from jax.experimental.pallas import tpu as pltpu
from jax.sharding import PartitionSpec as P

MESH = pl.DeviceIdType.MESH
BF = jnp.bfloat16
F32 = jnp.float32

SEG = 4
NZ = 8
NY = 8
GROUP = 4
SHARD = 12
SLOT = 16
BLOCK = GROUP * SHARD
ROWS = 64
MROWS = 16
MICRO = 4
IMG = GROUP * ROWS
HEAD = 64
GH = 3
GW = GH * HEAD
PIECE = 2 * GW
D = 1536
HD = 768
LONG = NZ // 2
PARTS = (2, 2, 2, 2)
FIRST = [(0, -1), (1, -1)]
BEFORE = [(0, 0), (-1, 0), (0, 1), (1, 0), (0, 2), (2, -1), (0, 3), (-1, 1), (1, 1)]
MIDDLE = [[(-1, 2), (2, 0), (3, -1), (1, 2)], [(3, 0), (2, 2)], [(3, 2)], []]
AFTER = [[(-1, 3), (1, 3), (2, 1)], [(2, 3), (3, 1)], [(3, 3)], []]


def kernel(
    x_hbm, stale_hbm, owner_ref, live_ref, gain_hbm, qkg_hbm, wqkv_hbm, wout_hbm,
    out_ref,
    x_ref, stale_ref, gain_ref, qkg_ref, wqkv_ref, wout_ref,
    wsend, stg, blk, w, stsend, st, gains, qkgs, xs, rs_out, rs_in, own_part,
    in_sem, wst_s, wst_r, g_s, g_r, qg_s, qg_r, st_s, st_r, y_s, y_r,
    ring_s, ring_r, m_s, m_r, rs_s, rs_r, ag_s, ag_r,
):
    c = lax.axis_index("segment")
    p = lax.axis_index("patch")
    image = p // GROUP
    j = p % GROUP
    core = p % 2
    y = (p // 2) % NY
    z = p // (2 * NY)
    yp = y // 2
    zh = z // 4
    mate = p + 1 - 2 * core

    def dev(seg, patch):
        return (seg, patch)

    def patch_of(zz, yy, cc):
        return zz * (2 * NY) + yy * 2 + cc

    inputs = [
        pltpu.make_async_copy(src, dst, in_sem.at[n])
        for n, (src, dst) in enumerate(
            [
                (wqkv_hbm, wqkv_ref), (wout_hbm, wout_ref), (stale_hbm, stale_ref),
                (gain_hbm, gain_ref), (qkg_hbm, qkg_ref), (x_hbm, x_ref),
            ]
        )
    ]
    for copy in inputs:
        copy.start()

    barrier = pltpu.get_barrier_semaphore()
    partners = []
    for dz in range(1, NZ):
        for low in range(2):
            partners.append(dev(c, patch_of((z + dz) % NZ, y, low)))
    for dc in range(SEG):
        for dj in range(GROUP):
            if dc or dj:
                partners.append(dev((c + dc) % SEG, image * GROUP + (j + dj) % GROUP))
    for dy in range(1, NY // 2):
        pair = (yp + dy) % (NY // 2)
        for low in range(4):
            partners.append(dev(c, z * (2 * NY) + pair * 4 + low))
    for partner in partners:
        pl.semaphore_signal(barrier, inc=1, device_id=partner, device_id_type=MESH)

    wsend[...] = jnp.zeros_like(wsend)
    inputs[0].wait()
    inputs[1].wait()
    for g in range(SEG):
        for part in range(3):
            wsend[part // 2, g, 0:SHARD, part % 2 * GW : (part % 2 + 1) * GW] = wqkv_ref[
                :, part * HD + g * GW : part * HD + (g + 1) * GW
            ]
        wsend[1, g, 0:SHARD, GW:] = wout_ref[:, g * GW : (g + 1) * GW]
    pl.semaphore_wait(barrier, len(partners))

    def remote(src, dst, ss, rs, device):
        return pltpu.make_async_remote_copy(
            src_ref=src, dst_ref=dst, send_sem=ss, recv_sem=rs,
            device_id=device, device_id_type=MESH,
        )

    holder = [2 * (1 - zh) + c % 2, 2 * zh + c % 2]
    holds_a = y % 2 != zh

    def stage(d, piece):
        g = (c + d) % SEG
        return remote(
            wsend.at[piece, g], stg.at[c // 2, j], wst_s.at[d, piece], wst_r.at[c // 2],
            dev(g, image * GROUP + holder[piece]),
        )

    for d in (2, 1, 3, 0):
        for piece in range(2):
            if d:
                stage(d, piece).start()
                continue

            @pl.when(j == holder[piece])
            def _():
                pltpu.make_async_copy(wsend.at[piece, c], stg.at[c // 2, j], wst_r.at[c // 2]).start()

            @pl.when(j != holder[piece])
            def _():
                stage(0, piece).start()

    inputs[3].wait()
    inputs[4].wait()
    for g in range(SEG):
        gains[c, g] = gain_ref[:, g * PIECE : (g + 1) * PIECE]
    qkgs[c] = qkg_ref[...]

    def gain_copy(d):
        return remote(gains.at[c], gains.at[c], g_s.at[d - 1], g_r.at[d - 1], dev((c + d) % SEG, p))

    def qkg_copy(d):
        return remote(qkg_ref, qkgs.at[c], qg_s.at[d - 1], qg_r.at[d - 1], dev((c + d) % SEG, p))

    across = p + 2 - 4 * (y % 2)
    j_across = (j + 2) % GROUP

    def stale_copy(d):
        g = (c + d) % SEG
        return remote(stsend.at[g], st.at[c, j], st_s.at[d], st_r.at[0], dev(g, p))

    def stale_rows(rest, index):
        return st.at[pl.ds(1, SEG - 1), index] if rest else st.at[0, index]

    def stale_across(rest):
        block = stale_rows(rest, j)
        return remote(block, block, st_s.at[4 + rest], st_r.at[1 + rest], dev(c, across))

    def stale_mate(rest):
        block = stale_rows(rest, j)
        return remote(block, block, st_s.at[6 + rest], st_r.at[3 + rest], dev(c, mate))

    def stale_mate_across(rest):
        block = stale_rows(rest, j_across)
        return remote(block, block, st_s.at[8 + rest], st_r.at[5 + rest], dev(c, mate))

    def stale_wait(block, n):
        pltpu.make_async_copy(block, block, st_r.at[n]).wait()

    a = lax.broadcasted_iota(jnp.int32, (BLOCK, GROUP * SLOT), 0)
    b = lax.broadcasted_iota(jnp.int32, (BLOCK, GROUP * SLOT), 1)
    pick = jnp.zeros((BLOCK, GROUP * SLOT), F32)
    for slot in range(GROUP):
        hit = (a - SHARD * slot == b - SLOT * slot) & (b >= SLOT * slot) & (b < SLOT * slot + SHARD)
        pick = jnp.where(hit, 1.0, pick)
    pick = pick.astype(BF)

    def compact(half):
        pltpu.make_async_copy(stg.at[half], stg.at[half], wst_r.at[half]).wait()
        blk[half] = jnp.dot(
            pick, stg[half].reshape(GROUP * SLOT, PIECE), preferred_element_type=F32
        ).astype(BF)

    def spread(half, piece, delta):
        s = core + 2 * half
        if piece == 0:
            target = patch_of(z, (y + delta) % NY, 0)
            dst, slot = w.at[s, 0, z, yp], yp
        else:
            target = patch_of((z + delta) % NZ, y, 1)
            dst, slot = w.at[s, 1, y, z % 4], z % 4
        return remote(blk.at[half], dst, y_s.at[half, delta], y_r.at[s, slot // 2], dev(c, target))

    def spread_all(s, act):
        half = s // 2
        for piece in range(2):

            @pl.when((core == s % 2) & (holds_a if piece == 0 else jnp.logical_not(holds_a)))
            def _():
                if s % 2 != piece:
                    act(spread(half, piece, 0))
                for delta in (4, 3, 5, 2, 6, 1, 7):
                    act(spread(half, piece, delta))

    def spread_start(s):
        half = s // 2
        if s % 2 == 0:

            @pl.when((core == 0) & holds_a)
            def _():
                pltpu.make_async_copy(blk.at[half], w.at[s, 0, z, yp], y_r.at[s, yp // 2]).start()

        else:

            @pl.when((core == 1) & jnp.logical_not(holds_a))
            def _():
                pltpu.make_async_copy(blk.at[half], w.at[s, 1, y, z % 4], y_r.at[s, z % 4 // 2]).start()

        spread_all(s, lambda copy: copy.start())

    place = jnp.where(core == 0, z, y)

    def neighbour(step):
        nz = jnp.where(core == 0, (z + step + NZ) % NZ, z)
        ny = jnp.where(core == 0, y, (y + step + NY) % NY)
        return dev(c, patch_of(nz, ny, core))

    near = jnp.where(core == 0, yp, z % 4)

    def ring_block(s, way, distance, q):
        size = GROUP // PARTS[s]
        source = (place - (1 - 2 * way) * distance + NZ) % NZ
        part = (near // size + q) % PARTS[s]
        return w.at[s, core, source, pl.ds(part * size, size)], part

    def arrival_index(s, way, distance, part):
        n = 2 * (distance - 1) + (way if distance < LONG else 0)
        return (NZ - 1) * sum(PARTS[:s]) + n * PARTS[s] + part

    def ring_copy(s, way, held, step, q):
        block, part = ring_block(s, way, held, q)
        arrival = ring_r.at[arrival_index(s, way, held + step, part)]
        return remote(block, block, ring_s.at[s], arrival, neighbour((1 - 2 * way) * step))

    def ring_wait(s, way, distance, q):
        block, part = ring_block(s, way, distance, q)
        pltpu.make_async_copy(block, block, ring_r.at[arrival_index(s, way, distance, part)]).wait()

    def to_mate(s, way, distance, q):
        block, _ = ring_block(s, way, distance, q)
        return remote(block, block, m_s.at[s], m_r.at[s], dev(c, mate))

    def arrivals(s):
        return [(way, distance) for distance in range(1, LONG + 1) for way in range(2) if distance < LONG or way == s % 2]

    def ring_start(s):
        for q in range(PARTS[s]):
            block, part = ring_block(s, 0, 0, q)
            size = GROUP // PARTS[s]
            for n in range(size // 2):
                half = part * size // 2 + n
                two = w.at[s, core, place, pl.ds(2 * half, 2)]
                pltpu.make_async_copy(two, two, y_r.at[s, half]).wait()
            for step in (2, 1):
                for way in range(2):
                    ring_copy(s, way, 0, step, q).start()
        for q in range(PARTS[s]):
            to_mate(s, 0, 0, q).start()

    def ring_forward(s):
        for q in range(PARTS[s]):
            for way in range(2):
                ring_wait(s, way, 2, q)
                if way == s % 2:
                    ring_copy(s, way, 2, 2, q).start()
                ring_copy(s, way, 2, 1, q).start()
        for q in range(PARTS[s]):
            for way in range(2):
                to_mate(s, way, 2, q).start()

    def ring_hand(s, distances):
        for way, distance in arrivals(s):
            if distance in distances:
                for q in range(PARTS[s]):
                    ring_wait(s, way, distance, q)
                    to_mate(s, way, distance, q).start()

    def stale_step(n):
        rest = n // 2
        if n % 2 == 0:
            if rest == 0:
                stale_wait(st.at[:, j], 0)
            stale_across(rest).start()
            stale_mate(rest).start()
        else:
            stale_wait(stale_rows(rest, j_across), 1 + rest)
            stale_mate_across(rest).start()

    def serve(plan):
        for s, t in plan:
            if s < 0:
                stale_step(t)
            elif t < 0:
                spread_start(s)
            elif t == 0:
                ring_start(s)
            elif t == 1:
                ring_forward(s)
            else:
                ring_hand(s, (1,) if t == 2 else (3, 4))

    compact(0)
    serve(FIRST)
    for d in range(1, SEG):
        gain_copy(d).start()
        qkg_copy(d).start()
    compact(1)

    inputs[2].wait()
    for g in range(SEG):
        for part in range(2):
            stsend[g, :, part * GW : (part + 1) * GW] = stale_ref[
                :, part * HD + g * GW : part * HD + (g + 1) * GW
            ]
    pltpu.make_async_copy(stsend.at[c], st.at[c, j], st_r.at[0]).start()
    for d in (2, 1, 3):
        stale_copy(d).start()
    inputs[5].wait()
    for g in range(SEG):
        xs[0, g] = x_ref[:, g * PIECE : (g + 1) * PIECE]

    serve(BEFORE)

    lane_g = lax.broadcasted_iota(jnp.int32, (1, GW), 1)
    head_of = [(lane_g >= h * HEAD) & (lane_g < (h + 1) * HEAD) for h in range(GH)]
    lane_w = lax.broadcasted_iota(jnp.int32, (1, 256), 1)
    head_in_window = [(lane_w >= 64 + h * HEAD) & (lane_w < 64 + (h + 1) * HEAD) for h in range(GH)]
    row = lax.broadcasted_iota(jnp.int32, (ROWS, IMG), 0)
    key_row = lax.broadcasted_iota(jnp.int32, (ROWS, IMG), 1)
    barred = jnp.zeros((ROWS, IMG), jnp.int32)
    live_count = live_ref[0]
    for m in range(MICRO):
        first = owner_ref[j * MICRO + m, image] * MROWS
        hit = (row >= m * MROWS) & (row < (m + 1) * MROWS) & (key_row >= first) & (key_row < first + MROWS)
        barred = jnp.where(hit, 1, barred)
    far_mask = jnp.where(barred == 1, 0.0, 1.0)
    far_mask = jnp.concatenate([far_mask] * GH, 0)
    own_r = lax.broadcasted_iota(jnp.int32, (ROWS, ROWS), 0)
    own_k = lax.broadcasted_iota(jnp.int32, (ROWS, ROWS), 1)
    own_mask = jnp.zeros((ROWS, ROWS), F32)
    for m in range(MICRO):
        lo, hi = m * MROWS, (m + 1) * MROWS
        own_mask = jnp.where((own_r >= lo) & (own_r < hi) & (own_k >= lo) & (own_k < hi), 1.0, own_mask)
    own_mask = jnp.concatenate([own_mask] * GH, 0)
    row1 = lax.broadcasted_iota(jnp.int32, (ROWS, 1), 0)
    live_rows = jnp.where(row1 < live_count * MROWS, 1.0, 0.0)
    live_rows = jnp.concatenate([live_rows] * GH, 0)

    def head_norm(part, gain_row):
        squares = part * part
        scale = jnp.zeros_like(part)
        for h in range(GH):
            mean = jnp.sum(jnp.where(head_of[h], squares, 0.0), -1, keepdims=True) * (1.0 / HEAD)
            scale = jnp.where(head_of[h], lax.rsqrt(mean + 1e-06), scale)
        return part * scale * gain_row

    def nt(lhs, rhs):
        return lax.dot_general(lhs, rhs, (((1,), (1,)), ((), ())), preferred_element_type=F32)

    def w_b_rows(s, g):
        return jnp.concatenate(
            [w[s, 1, 2 * b + g // 2, 2 * (g % 2) + zz] for zz in range(2) for b in range(NY // 2)], 0
        )

    def chain_front(s):
        other = 1 - core
        pltpu.make_async_copy(w.at[s, other], w.at[s, other], m_r.at[s]).wait()
        if s == 0:
            for d in range(1, SEG):
                src = (c + SEG - d) % SEG
                pltpu.make_async_copy(gains.at[src], gains.at[src], g_r.at[d - 1]).wait()
                pltpu.make_async_copy(qkg_ref, qkgs.at[src], qg_r.at[d - 1]).wait()
        product_a = jnp.zeros((ROWS, PIECE), F32)
        product_b = jnp.zeros((ROWS, PIECE), F32)
        squares = jnp.zeros((ROWS, 1), F32)
        for d in (0, 1, 3, 2):
            g = (c + SEG - d) % SEG
            if s and d:
                pltpu.make_async_copy(xs.at[s, g], xs.at[s, g], ag_r.at[s - 1, d - 1]).wait()
            x = xs[s, g].astype(F32)
            squares = squares + jnp.sum(x * x, -1, keepdims=True)
            scaled = (x * gains[s, g]).astype(BF)
            w_a = w[s, 0, pl.ds(2 * g, 2)].reshape(PIECE, PIECE)
            product_a = product_a + jnp.dot(scaled, w_a, preferred_element_type=F32)
            product_b = product_b + jnp.dot(scaled, w_b_rows(s, g), preferred_element_type=F32)
        inverse = lax.rsqrt(squares * (1.0 / D) + 1e-06)
        qk = (product_a * inverse).astype(BF).astype(F32)
        value = (product_b * inverse).astype(BF)
        gq = qkgs[s, 0:1, :]
        gk = qkgs[s, 1:2, :]
        query = head_norm(qk[:, :GW], jnp.concatenate([gq] * GH, 1))
        key = head_norm(qk[:, GW:], jnp.concatenate([gk] * GH, 1)).astype(BF)
        query = query.astype(BF).astype(F32)
        stacked = jnp.concatenate([jnp.where(head_of[h], query, 0.0) for h in range(GH)], 0).astype(BF)
        if s < 2:
            stale_wait(stale_rows(s, j + 1 - 2 * core), 3 + s)
            stale_wait(stale_rows(s, j_across + 1 - 2 * core), 5 + s)
        kv = st[s].reshape(IMG, PIECE)
        scale = HEAD**-0.5
        far = jnp.exp(nt(stacked, kv[:, :GW]) * scale) * far_mask
        own = jnp.exp(nt(stacked, key) * scale) * own_mask
        total = jnp.sum(far, -1, keepdims=True) + jnp.sum(own, -1, keepdims=True)
        value_window = jnp.concatenate([jnp.zeros((ROWS, 64), F32), value[:, :GW].astype(F32)], 1).astype(BF)
        weighted = jnp.dot(far.astype(BF), kv[:, PIECE - 256 :], preferred_element_type=F32)
        weighted = weighted + jnp.dot(own.astype(BF), value_window, preferred_element_type=F32)
        weighted = weighted * (live_rows / total)
        attended = jnp.zeros((ROWS, 256), F32)
        for h in range(GH):
            attended = jnp.where(head_in_window[h], weighted[h * ROWS : (h + 1) * ROWS], attended)
        attended = attended.astype(BF)
        for d in (2, 1, 3, 0):
            g = (c + d) % SEG
            part = nt(attended, w_b_rows(s, g)[:, PIECE - 256 :])
            if d:
                rs_out[s, d - 1] = part.astype(BF)
                rs_copy(s, d).start()
            else:
                own_part[...] = part

    def rs_copy(s, d):
        return remote(
            rs_out.at[s, d - 1], rs_in.at[s, d - 1], rs_s.at[s], rs_r.at[s],
            dev((c + d) % SEG, p),
        )

    def ag_copy(s, d):
        return remote(
            xs.at[s + 1, c], xs.at[s + 1, c], ag_s.at[s], ag_r.at[s, d - 1],
            dev((c + d) % SEG, p),
        )

    def last_copy():
        return remote(
            xs.at[SEG, c], xs.at[SEG, c], ag_s.at[SEG - 1], ag_r.at[SEG - 1, (2 * SEG - 2 - c) % SEG],
            dev(SEG - 1, p),
        )

    def chain_back(s):
        pltpu.make_async_copy(rs_in.at[s], rs_in.at[s], rs_r.at[s]).wait()
        total = own_part[...]
        for d in range(1, SEG):
            total = total + rs_in[s, d - 1].astype(F32)
        xs[s + 1, c] = (xs[s, c].astype(F32) + total).astype(BF)
        if s + 1 < SEG:
            for d in (2, 1, 3):
                ag_copy(s, d).start()
        else:

            @pl.when(c != SEG - 1)
            def _():
                last_copy().start()

    for s in range(SEG):
        chain_front(s)
        serve(MIDDLE[s])
        chain_back(s)
        serve(AFTER[s])

    @pl.when(c == SEG - 1)
    def _():
        for d in range(1, SEG):
            src = (c + SEG - d) % SEG
            pltpu.make_async_copy(xs.at[SEG, src], xs.at[SEG, src], ag_r.at[SEG - 1, d - 1]).wait()

    for g in range(SEG):
        out_ref[0, :, g * PIECE : (g + 1) * PIECE] = xs[c + 1, g]

    for d in range(SEG):
        for piece in range(2):
            if d:
                stage(d, piece).wait_send()
            else:

                @pl.when(j != holder[piece])
                def _():
                    stage(0, piece).wait_send()

    for d in range(1, SEG):
        gain_copy(d).wait_send()
        qkg_copy(d).wait_send()
        stale_copy(d).wait_send()
    for rest in range(2):
        stale_across(rest).wait_send()
        stale_mate(rest).wait_send()
        stale_mate_across(rest).wait_send()
    for s in range(SEG):
        spread_all(s, lambda copy: copy.wait_send())
    for s in range(SEG):
        for block, sem in (
            (w.at[s, core, pl.ds(0, NZ - 1)], ring_s), (w.at[s, core], m_s), (rs_out.at[s], rs_s), (rs_out.at[s], ag_s)
        ):
            if sem is not ag_s or s + 1 < SEG:
                pltpu.make_async_copy(block, block, sem.at[s]).wait()

    @pl.when(c != SEG - 1)
    def _():
        last_copy().wait_send()


def per_device(x_in, stale_kv, owner, live, gain, qk_gain, w_qkv, w_out):
    vmem = pl.BlockSpec(memory_space=pltpu.VMEM)
    hbm = pl.BlockSpec(memory_space=pltpu.HBM)
    smem = pl.BlockSpec(memory_space=pltpu.SMEM)
    dma = pltpu.SemaphoreType.DMA
    return pl.pallas_call(
        kernel,
        out_shape=jax.ShapeDtypeStruct((1, ROWS, D), BF),
        in_specs=[hbm, hbm, smem, smem, hbm, hbm, hbm, hbm],
        out_specs=vmem,
        scratch_shapes=[
            pltpu.VMEM((ROWS, D), BF),
            pltpu.VMEM((ROWS, D), BF),
            pltpu.VMEM((1, D), F32),
            pltpu.VMEM((2, HEAD), F32),
            pltpu.VMEM((SHARD, 3 * HD), BF),
            pltpu.VMEM((SHARD, HD), BF),
            pltpu.VMEM((2, SEG, SLOT, PIECE), BF),
            pltpu.VMEM((2, GROUP, SLOT, PIECE), BF),
            pltpu.VMEM((2, BLOCK, PIECE), BF),
            pltpu.VMEM((SEG, 2, NZ, NY // 2, BLOCK, PIECE), BF),
            pltpu.VMEM((SEG, ROWS, PIECE), BF),
            pltpu.VMEM((SEG, GROUP, ROWS, PIECE), BF),
            pltpu.VMEM((SEG, SEG, 1, PIECE), F32),
            pltpu.VMEM((SEG, 2, HEAD), F32),
            pltpu.VMEM((SEG + 1, SEG, ROWS, PIECE), BF),
            pltpu.VMEM((SEG, SEG - 1, ROWS, PIECE), BF),
            pltpu.VMEM((SEG, SEG - 1, ROWS, PIECE), BF),
            pltpu.VMEM((ROWS, PIECE), F32),
            dma((6,)), dma((SEG, 2)), dma((2,)),
            dma((SEG - 1,)), dma((SEG - 1,)), dma((SEG - 1,)), dma((SEG - 1,)),
            dma((10,)), dma((7,)),
            dma((2, NY)), dma((SEG, 2)),
            dma((SEG,)), dma(((NZ - 1) * sum(PARTS),)), dma((SEG,)), dma((SEG,)),
            dma((SEG,)), dma((SEG,)), dma((SEG,)), dma((SEG, SEG - 1)),
        ],
        compiler_params=pltpu.CompilerParams(
            collective_id=0, has_side_effects=True, vmem_limit_bytes=62 * 2**20
        ),
    )(x_in, stale_kv[0], owner.T, live, gain, qk_gain[0], w_qkv[0], w_out[0].T)


def solution(mesh):
    in_specs = (
        P("patch", None),
        P("segment", "patch", None),
        P(),
        P("patch"),
        P("segment", None),
        P("segment", None, None),
        P("segment", "patch", None),
        P("segment", None, "patch"),
    )
    return jax.shard_map(
        per_device, mesh=mesh, in_specs=in_specs, out_specs=P("segment", "patch", None), check_vma=False
    )
```
